512 devices in a mesh: lat: 32 (over x, z_lo), lon: 16 (over y, z_hi, core).
Axes of the slice: x: 4, y: 4, z: 16 (z_hi: 2, z_lo: 8; z = z_hi * 8 + z_lo), core: 2. Of those that a mesh axis runs over, the one named last changes fastest.
Arguments:
- thermal_anomaly_field: float32 [16, 1024, 2048], P(None, 'lat', 'lon'), may hold values from -6 to 6
- seawater_salt_anomaly: float32 [16, 1024, 2048], P(None, 'lat', 'lon'), may hold values from -6 to 6
- longitude_flow_speed: float32 [16, 1024, 2048], P(None, 'lat', 'lon'), may hold values from -0.45 to 0.45
- latitude_flow_speed: float32 [16, 1024, 2048], P(None, 'lat', 'lon'), may hold values from -0.45 to 0.45
- marine_profile_flag: int32 [1024, 2048], P('lat', 'lon'), may hold values 0 or 1
- submerged_layer_tally: int32 [1024, 2048], P('lat', 'lon'), may hold values from 1 to 16
Outputs:
- temperature_next: float32 [16, 1024, 2048], P(None, 'lat', 'lon')
- salinity_next: float32 [16, 1024, 2048], P(None, 'lat', 'lon')
- east_next: float32 [16, 1024, 2048], P(None, 'lat', 'lon')
- north_next: float32 [16, 1024, 2048], P(None, 'lat', 'lon')
The draws below stay inside these ranges and needn't reach their ends.
All inputs are finite; a program needn't handle non-finite values. No bound on the sum of `marine_profile_flag` on one device may be relied on, other than what follows from the above.
Results may differ from the reference program's by a relative error of at most 0.0003.
Values sent between devices are 32-bit elements; how exact they have to be, the bound alone decides.
No kernel may reach another device: no remote copies, remote signals or barrier semaphores. Data moves between devices by JAX's collectives and lax.ppermute only.
A program may use at most 64 MiB of HBM per device.

```python
import jax
import jax.numpy as jnp
from jax import lax

CY = 32
LAYER_TOTAL = 16
LONGITUDE_SPAN = 2048
LATITUDE_SPAN = 1024
N_LAT = 32


def plant(array, key, low, largest):
    extent = array.shape
    spot = [jax.random.randint(jax.random.fold_in(key, axis), (), 0, extent[axis]) for axis in range(len(extent))]
    array = array.at[tuple(spot)].set(low)
    longest = extent.index(max(extent))
    spot[longest] = (spot[longest] + 1) % extent[longest]
    return array.at[tuple(spot)].set(largest)


def levels(stream_key, shape, shards, smallest, largest):
    level = 1.0
    for dim, shards_of in shards:
        steps = jax.random.uniform(jax.random.fold_in(jax.random.fold_in(stream_key, 6), dim), (shards_of,), jnp.float32, smallest / len(shards), largest / len(shards))
        level = level * jnp.repeat(jnp.exp(steps), shape[dim] // shards_of).reshape((-1,) + (1,) * (len(shape) - 1 - dim))
    return level


def bell_draw(own_key, dims, scale, most, pieces=(), kind=jnp.bfloat16):
    loudness = levels(own_key, dims, pieces, -0.22, 0.18) if pieces else 1.0
    values = jax.random.normal(own_key, dims, jnp.float32) * scale * loudness
    return jnp.minimum(jnp.maximum(values, -most), most).astype(kind)


def setup_inputs(seed: int = 0) -> dict:
    keys = jax.random.split(jax.random.key(seed), 7)
    thermal_anomaly_field = bell_draw(keys[0], (LAYER_TOTAL, LATITUDE_SPAN, LONGITUDE_SPAN), 1.0, 6.0, ((1, 32), (2, 16)), jnp.float32)
    seawater_salt_anomaly = bell_draw(keys[1], (LAYER_TOTAL, LATITUDE_SPAN, LONGITUDE_SPAN), 1.0, 6.0, ((1, 32), (2, 16)), jnp.float32)
    longitude_flow_speed = jnp.clip(jax.random.uniform(keys[2], (LAYER_TOTAL, LATITUDE_SPAN, LONGITUDE_SPAN), jnp.float32, -0.45, 0.45) * levels(keys[2], (LAYER_TOTAL, LATITUDE_SPAN, LONGITUDE_SPAN), ((1, 32), (2, 16)), -0.4, 0.0), -0.45, 0.45)
    latitude_flow_speed = jnp.clip(jax.random.uniform(keys[3], (LAYER_TOTAL, LATITUDE_SPAN, LONGITUDE_SPAN), jnp.float32, -0.45, 0.45) * levels(keys[3], (LAYER_TOTAL, LATITUDE_SPAN, LONGITUDE_SPAN), ((1, 32), (2, 16)), -0.4, 0.0), -0.45, 0.45)
    marine_profile_flag = plant((jax.random.randint(keys[4], (LATITUDE_SPAN, LONGITUDE_SPAN), 0, 5) < 4).astype(jnp.int32), jax.random.fold_in(keys[4], 1), 0, 1)
    submerged_layer_tally = plant(jax.random.randint(keys[5], (LATITUDE_SPAN, LONGITUDE_SPAN), 1, LAYER_TOTAL + 1), jax.random.fold_in(keys[5], 1), 1, LAYER_TOTAL).astype(jnp.int32)
    return dict(thermal_anomaly_field=thermal_anomaly_field, seawater_salt_anomaly=seawater_salt_anomaly, longitude_flow_speed=longitude_flow_speed, latitude_flow_speed=latitude_flow_speed, marine_profile_flag=marine_profile_flag, submerged_layer_tally=submerged_layer_tally)


MIXING = 0.2
VISCOSITY = 0.05
ROTATION = 0.3


def row_angles(row_ids, total_rows):
    mirrored = jnp.where(row_ids >= total_rows, 2 * total_rows - 1 - row_ids, row_ids)
    return ROTATION * (2.0 * (mirrored.astype(jnp.float32) + 0.5) / total_rows - 1.0)


def substep(padded, angles):
    planes = padded.shape[0]
    layer_ordinal_index = (planes - 1) // 4
    profile_layer_height = padded[planes - 1]
    ordinal = jnp.arange(layer_ordinal_index, dtype=jnp.float32)[:, None, None]
    wetness = (ordinal < profile_layer_height[None]).astype(jnp.float32)
    heat = padded[:layer_ordinal_index]
    saltiness = padded[layer_ordinal_index:2 * layer_ordinal_index]
    zonal = padded[2 * layer_ordinal_index:3 * layer_ordinal_index]
    meridional = padded[3 * layer_ordinal_index:4 * layer_ordinal_index]
    inside = wetness[:, 1:-1, 1:-1]
    east_face = 0.5 * (zonal[:, 1:-1, :-1] + zonal[:, 1:-1, 1:]) * (wetness[:, 1:-1, :-1] * wetness[:, 1:-1, 1:])
    north_face = 0.5 * (meridional[:, :-1, 1:-1] + meridional[:, 1:, 1:-1]) * (wetness[:, :-1, 1:-1] * wetness[:, 1:, 1:-1])

    def transport(quantity):
        across = jnp.maximum(east_face, 0.0) * quantity[:, 1:-1, :-1] + jnp.minimum(east_face, 0.0) * quantity[:, 1:-1, 1:]
        upward = jnp.maximum(north_face, 0.0) * quantity[:, :-1, 1:-1] + jnp.minimum(north_face, 0.0) * quantity[:, 1:, 1:-1]
        return (across[:, :, 1:] - across[:, :, :-1]) + (upward[:, 1:, :] - upward[:, :-1, :])

    def mixing(centre):
        vertical = MIXING * (centre[1:] - centre[:-1]) * (inside[1:] * inside[:-1])
        zeroes = jnp.zeros_like(centre[:1])
        return jnp.concatenate([vertical, zeroes], 0) - jnp.concatenate([zeroes, vertical], 0)

    def spread(quantity, centre):
        zonal_part = (quantity[:, 1:-1, 2:] - centre) * wetness[:, 1:-1, 2:] + (quantity[:, 1:-1, :-2] - centre) * wetness[:, 1:-1, :-2]
        merid_part = (quantity[:, 2:, 1:-1] - centre) * wetness[:, 2:, 1:-1] + (quantity[:, :-2, 1:-1] - centre) * wetness[:, :-2, 1:-1]
        return zonal_part + merid_part

    def tracer(quantity):
        centre = quantity[:, 1:-1, 1:-1]
        return inside * (centre - transport(quantity) + mixing(centre))

    zonal_c = zonal[:, 1:-1, 1:-1]
    merid_c = meridional[:, 1:-1, 1:-1]
    zonal_a = zonal_c - transport(zonal) + VISCOSITY * spread(zonal, zonal_c)
    merid_a = merid_c - transport(meridional) + VISCOSITY * spread(meridional, merid_c)
    cosine = jnp.cos(angles)[None, :, None]
    sine = jnp.sin(angles)[None, :, None]
    zonal_n = inside * (cosine * zonal_a + sine * merid_a)
    merid_n = inside * (cosine * merid_a - sine * zonal_a)
    return jnp.concatenate([tracer(heat), tracer(saltiness), zonal_n, merid_n, profile_layer_height[None, 1:-1, 1:-1]], 0)


def fold_signs(planes):
    layer_ordinal_index = (planes - 1) // 4
    ordinal = jnp.arange(planes)
    return jnp.where((ordinal >= 2 * layer_ordinal_index) & (ordinal < 4 * layer_ordinal_index), -1.0, 1.0).astype(jnp.float32)[:, None, None]


def extend_global(marine_condition_bundle):
    wrapped = jnp.concatenate([marine_condition_bundle[:, :, -1:], marine_condition_bundle, marine_condition_bundle[:, :, :1]], 2)
    southern = jnp.zeros_like(wrapped[:, :1])
    northern = wrapped[:, -1:, ::-1] * fold_signs(marine_condition_bundle.shape[0])
    return jnp.concatenate([southern, wrapped, northern], 1)


def reference(thermal_anomaly_field, seawater_salt_anomaly, longitude_flow_speed, latitude_flow_speed, marine_profile_flag, submerged_layer_tally):
    profile_layer_height = (marine_profile_flag * submerged_layer_tally).astype(jnp.float32)[None]
    marine_condition_bundle = jnp.concatenate([thermal_anomaly_field, seawater_salt_anomaly, longitude_flow_speed, latitude_flow_speed, profile_layer_height], 0)
    planes = marine_condition_bundle.shape[0]
    total_rows = CY * N_LAT
    for repeat in range(2):
        padded = extend_global(marine_condition_bundle)

        def one_block(block_id):
            start = (block_id * CY).astype(jnp.int32)
            section = lax.dynamic_slice_in_dim(padded, start, CY + 2, 1)
            row_ids = start + jnp.arange(CY, dtype=jnp.int32)
            return substep(section, row_angles(row_ids, total_rows))

        blocks = lax.map(one_block, jnp.arange(N_LAT, dtype=jnp.int32))
        marine_condition_bundle = jnp.transpose(blocks, (1, 0, 2, 3)).reshape(planes, total_rows, marine_condition_bundle.shape[2])
    return (marine_condition_bundle[:LAYER_TOTAL], marine_condition_bundle[LAYER_TOTAL:2 * LAYER_TOTAL], marine_condition_bundle[2 * LAYER_TOTAL:3 * LAYER_TOTAL], marine_condition_bundle[3 * LAYER_TOTAL:4 * LAYER_TOTAL])
```

```python
import jax
import jax.numpy as jnp
from jax import lax
from jax.experimental import pallas as pl
from jax.experimental.pallas import tpu as pltpu
from jax.sharding import PartitionSpec as P

MIXING = 0.2
VISCOSITY = 0.05
ROTATION = 0.3
LEVELS = 16
ROWS = 32
LANES = 128
N_LAT = 32
N_LON = 16
BLOCK = 8
ROW_MSG = 136
COL_MSG = 48
EDGE_MSG = COL_MSG + ROW_MSG + 8


def near_lon(lat, lon):
    return lat, lon ^ 1


def far_lon(lat, lon):
    return lat, (lon + 1) % N_LON if lon % 2 else (lon - 1) % N_LON


def even_lat(lat, lon):
    return lat ^ 1, lon


def odd_lat(lat, lon):
    if lat == N_LAT - 1:
        return lat, N_LON - 1 - lon
    return (lat + 1 if lat % 2 else lat - 1), lon


def is_edge(lat):
    return lat > 0 and lat % BLOCK in (0, BLOCK - 1)


def pairs(where_to, member):
    found = []
    for lat in range(N_LAT):
        for lon in range(N_LON):
            if member(lat):
                to_lat, to_lon = where_to(lat, lon)
                found.append((lat * N_LON + lon, to_lat * N_LON + to_lon))
    return found


def send(array, where_to, member):
    return lax.ppermute(array, ("lat", "lon"), pairs(where_to, member))


def odd_or_diagonal(lat, lon):
    to = odd_lat(lat, lon)
    return far_lon(*to) if is_edge(lat) else to


def near_corner_relay(lat, lon):
    return far_lon(*near_lon(*odd_lat(lat, lon)))


def shift(x, by, axis=1):
    by = by % x.shape[axis]
    return x if by == 0 else pltpu.roll(x, by, axis)


def lanes_of(shape):
    return lax.broadcasted_iota(jnp.int32, shape, 1)


def position():
    return lax.axis_index("lat"), lax.axis_index("lon")


def pack_kernel(heat, salt, zonal, merid, flag, tally, row_even, row_odd, packed, col_near, col_far):
    lat, lon = position()
    lat_odd = lax.rem(lat, 2) == 1
    lon_odd = lax.rem(lon, 2) == 1
    depth = (flag[...] * tally[...]).astype(jnp.float32)
    lane = lanes_of((ROWS, LANES))
    group = lane >> 3
    pair = (lane & 7) >> 1
    west = jnp.zeros((ROWS, LANES), jnp.float32)
    east = west
    for f, field in enumerate((heat, salt, zonal, merid)):
        acc = jnp.zeros((ROWS, LANES), jnp.float32)
        for k in range(LEVELS):
            acc = jnp.where(group == k, shift(field[k], 8 * k + 2), acc)
        packed[f] = acc
        west = jnp.where(pair == f, shift(acc, 2 * f - 2), west)
        east = jnp.where(pair == f, shift(acc, 2 * f), east)
        for d in range(2):
            at = (d * 4 + f) * LEVELS
            top = field[:, ROWS - 1 - d, :]
            bottom = field[:, d, :]
            row_even[at : at + LEVELS, :] = jnp.where(lat_odd, bottom, top)
            row_odd[at : at + LEVELS, :] = jnp.where(lat_odd, top, bottom)
    short = lanes_of((8, LANES)) >> 1
    depth_west = jnp.zeros((8, LANES), jnp.float32)
    depth_east = depth_west
    for i in range(4):
        part = depth[8 * i : 8 * i + 8]
        depth_west = jnp.where(short == i, shift(part, 2 * i), depth_west)
        depth_east = jnp.where(short == i, shift(part, 2 * i + 2), depth_east)
    col_near[0:ROWS, :] = jnp.where(lon_odd, west, east)
    col_far[0:ROWS, :] = jnp.where(lon_odd, east, west)
    col_near[ROWS : ROWS + 8, :] = jnp.where(lon_odd, depth_west, depth_east)
    col_far[ROWS : ROWS + 8, :] = jnp.where(lon_odd, depth_east, depth_west)
    blank = jnp.zeros((4, LANES), jnp.float32)
    tops = jnp.concatenate([depth[31:32], depth[30:31], west[31:32], east[31:32], blank], 0)
    bottoms = jnp.concatenate([depth[0:1], depth[1:2], west[0:1], east[0:1], blank], 0)
    row_even[128:136, :] = jnp.where(lat_odd, bottoms, tops)
    row_odd[128:136, :] = jnp.where(lat_odd, tops, bottoms)


def relay_kernel(even, odd, near_corner, col_near, col_far, to_near, to_far, to_far_edge):
    _, lon = position()
    lon_odd = lax.rem(lon, 2) == 1
    blank = jnp.zeros((4, LANES), jnp.float32)
    info_even = even[128:136, :]
    info_odd = odd[128:136, :]

    def corners(row):
        return jnp.concatenate(
            [info_even[row : row + 1], info_odd[row : row + 1], info_even[0:1], info_odd[0:1], blank], 0
        )

    west, east = corners(2), corners(3)
    to_near[0:40, :] = col_near[...]
    to_near[40:48, :] = jnp.where(lon_odd, west, east)
    far_tile = jnp.where(lon_odd, east, west)
    to_far[0:40, :] = col_far[...]
    to_far[40:48, :] = far_tile
    to_far_edge[0:40, :] = col_far[...]
    to_far_edge[40:48, :] = far_tile
    to_far_edge[48:184, :] = odd[...]
    to_far_edge[184:192, :] = near_corner[...]


def reversed_lanes(x):
    lane = lanes_of(x.shape)
    for b in range(7):
        x = jnp.where((lane >> b) & 1 == 1, shift(x, 1 << b), shift(x, -(1 << b)))
    return x


def five_point(c, e, w, n, s, up, down, wet, wets, wet_up, wet_down, cosine, sine):
    wet_e, wet_w, wet_n, wet_s = (wet * x for x in wets)
    flow_e = 0.5 * (c[2] + e[2]) * wet_e
    flow_w = 0.5 * (c[2] + w[2]) * wet_w
    flow_n = 0.5 * (c[3] + n[3]) * wet_n
    flow_s = 0.5 * (c[3] + s[3]) * wet_s

    def gain(f, viscosity):
        east = (jnp.maximum(flow_e, 0.0) * c[f] + jnp.minimum(flow_e, 0.0) * e[f]) - viscosity * wet_e * (e[f] - c[f])
        west = (jnp.maximum(flow_w, 0.0) * w[f] + jnp.minimum(flow_w, 0.0) * c[f]) - viscosity * wet_w * (c[f] - w[f])
        north = (jnp.maximum(flow_n, 0.0) * c[f] + jnp.minimum(flow_n, 0.0) * n[f]) - viscosity * wet_n * (n[f] - c[f])
        south = (jnp.maximum(flow_s, 0.0) * s[f] + jnp.minimum(flow_s, 0.0) * c[f]) - viscosity * wet_s * (c[f] - s[f])
        return c[f] - ((east - west) + (north - south))

    def tracer(f):
        mixed = MIXING * ((up[f] - c[f]) * (wet * wet_up) - (c[f] - down[f]) * (wet * wet_down))
        return wet * (gain(f, 0.0) + mixed)

    ua, va = gain(2, VISCOSITY), gain(3, VISCOSITY)
    return [tracer(0), tracer(1), wet * (cosine * ua + sine * va), wet * (cosine * va - sine * ua)]


def north_of(x, last):
    return jnp.concatenate([x[1:], last], 0)


def south_of(x, first):
    return jnp.concatenate([first, x[:-1]], 0)


def as_wet(mask):
    return jnp.where(mask, 1.0, 0.0)


def step_kernel(
    heat, salt, zonal, merid, flag, tally, packed, angles, even, odd, near, far, far_edge,
    heat_out, salt_out, zonal_out, merid_out, mid,
):
    lat, lon = position()
    lat_odd = lax.rem(lat, 2) == 1
    lon_odd = lax.rem(lon, 2) == 1
    at_top = lat == N_LAT - 1
    run = lax.rem(lat, BLOCK)
    edge = jnp.logical_and(lat > 0, jnp.logical_or(run == 0, run == BLOCK - 1))
    fields = (heat, salt, zonal, merid)
    lane = lanes_of((ROWS, LANES))
    place = lane & 7
    level = (lane >> 3).astype(jnp.float32)
    lane1 = lanes_of((1, LANES))
    place1 = lane1 & 7
    depth = (flag[...] * tally[...]).astype(jnp.float32)
    cosine, sine = angles[0:32, :], angles[32:64, :]

    signs = jnp.where(jnp.logical_and(at_top, place1 >= 4), -1.0, 1.0)

    def swap_pair(x):
        return jnp.where(lane1 & 1 == 1, shift(x, 1), shift(x, -1)) * signs

    def unfold_info(info):
        drow, west, east = info[0:1], info[2:3], info[3:4]
        return (
            jnp.where(at_top, reversed_lanes(drow), drow),
            jnp.where(at_top, swap_pair(east), west),
            jnp.where(at_top, swap_pair(west), east),
        )

    odd_rows = jnp.where(edge, far_edge[48:184, :], odd[...])
    turned = reversed_lanes(odd_rows)
    row_field = (lax.broadcasted_iota(jnp.int32, (ROW_MSG, LANES), 0) >> 4) & 3
    below = lax.broadcasted_iota(jnp.int32, (ROW_MSG, LANES), 0) < 128
    turned = jnp.where(jnp.logical_and(below, row_field >= 2), -turned, turned)
    odd_rows = jnp.where(at_top, turned, odd_rows)
    even_rows = even[...]
    south_rows = jnp.where(lat_odd, even_rows, odd_rows)
    north_rows = jnp.where(lat_odd, odd_rows, even_rows)
    far_cols = jnp.where(edge, far_edge[0:48, :], far[...])
    near_cols = near[...]
    west_cols = jnp.where(lon_odd, near_cols, far_cols)
    east_cols = jnp.where(lon_odd, far_cols, near_cols)

    q_depth, q_west, q_east = unfold_info(odd[128:136, :])
    s_depth, s_west, s_east = unfold_info(far_edge[184:192, :])
    far_corner = jnp.where(lon_odd, q_west, q_east)
    near_corner = jnp.where(lon_odd, s_east, s_west)
    west_odd = jnp.where(edge, jnp.where(lon_odd, near_corner, far_corner), west_cols[41:42])
    east_odd = jnp.where(edge, jnp.where(lon_odd, far_corner, near_corner), east_cols[41:42])
    west_odd_depth = jnp.where(edge, jnp.where(lon_odd, s_depth, q_depth), west_cols[43:44])
    east_odd_depth = jnp.where(edge, jnp.where(lon_odd, q_depth, s_depth), east_cols[43:44])

    def by_side(even_part, odd_part):
        return jnp.where(lat_odd, even_part, odd_part), jnp.where(lat_odd, odd_part, even_part)

    sw, nw = by_side(west_cols[40:41], west_odd)
    se, ne = by_side(east_cols[40:41], east_odd)
    sw_d, nw_d = by_side(west_cols[42:43], west_odd_depth)
    se_d, ne_d = by_side(east_cols[42:43], east_odd_depth)
    corner_depth = [(x[:, 127:128], y[:, 0:1]) for x, y in ((sw_d, se_d), (nw_d, ne_d))]

    cols, cols_s, cols_n = [], [], []
    for f in range(4):
        own = packed[f]
        x = jnp.where(place < 2, own, shift(own, 4))
        x = jnp.where((place >> 1) == 1, shift(east_cols[0:32], 2 - 2 * f), x)
        x = jnp.where((place >> 1) == 2, shift(west_cols[0:32], 4 - 2 * f), x)
        cols.append(x)
        for out, w, e in ((cols_s, sw, se), (cols_n, nw, ne)):
            out.append(
                jnp.where(place1 == 5, shift(w, 4 - 2 * f), jnp.where(place1 == 2, shift(e, 2 - 2 * f), 0.0))
            )
    west_d = jnp.concatenate([shift(west_cols[32:40], 4 - 2 * i) for i in range(4)], 0)
    east_d = jnp.concatenate([shift(east_cols[32:40], 2 - 2 * i) for i in range(4)], 0)
    col_depth = jnp.where(lane < 2, shift(depth, 2), shift(depth, 6))
    col_depth = jnp.where((lane >> 1) == 1, east_d, col_depth)
    col_depth = jnp.where((lane >> 1) == 2, west_d, col_depth)
    col_depth = jnp.where(lane < 8, col_depth, 0.0)
    for b in (8, 16, 32, 64):
        col_depth = col_depth + shift(col_depth, b)
    corner_rows = [
        jnp.where(place1 == 5, w, jnp.where(place1 == 2, e, 0.0)) for w, e in corner_depth
    ]

    wets = [
        as_wet(level < x)
        for x in (
            shift(col_depth, -1),
            shift(col_depth, 1),
            north_of(col_depth, corner_rows[1]),
            south_of(col_depth, corner_rows[0]),
        )
    ]
    cols_mid = five_point(
        cols,
        [shift(x, -1) for x in cols],
        [shift(x, 1) for x in cols],
        [north_of(x, y) for x, y in zip(cols, cols_n)],
        [south_of(x, y) for x, y in zip(cols, cols_s)],
        [shift(x, -8) for x in cols[:2]],
        [shift(x, 8) for x in cols[:2]],
        as_wet(level < col_depth),
        wets,
        as_wet(level + 1.0 < col_depth),
        as_wet(jnp.logical_and(lane >= 8, level - 1.0 < col_depth)),
        cosine,
        sine,
    )

    lane16 = lanes_of((LEVELS, LANES))
    sub16 = lax.broadcasted_iota(jnp.int32, (LEVELS, LANES), 0)
    lev16 = sub16.astype(jnp.float32)

    def halo_row(rows, corner_cols, corner_d, own_row, north, at):
        c = [rows[f * 16 : f * 16 + 16] for f in range(4)]
        beyond = [rows[64 + f * 16 : 64 + f * 16 + 16] for f in range(4)]
        inner = [x[:, own_row, :] for x in fields]
        d0, d1, d_in = rows[128:129], rows[129:130], depth[own_row : own_row + 1]
        d_w = jnp.where(lane1 == 0, corner_d[0], shift(d0, 1))
        d_e = jnp.where(lane1 == 127, corner_d[1], shift(d0, -1))
        e, w = [], []
        for f in range(4):
            spread_out = jnp.broadcast_to(corner_cols[f], (LEVELS, LANES))
            at_w = jnp.sum(jnp.where(lane16 == 8 * sub16 + 5, spread_out, 0.0), axis=1, keepdims=True)
            at_e = jnp.sum(jnp.where(lane16 == 8 * sub16 + 2, spread_out, 0.0), axis=1, keepdims=True)
            w.append(jnp.where(lane16 == 0, at_w, shift(c[f], 1)))
            e.append(jnp.where(lane16 == 127, at_e, shift(c[f], -1)))
        n, s, d_n, d_s = (beyond, inner, d1, d_in) if north else (inner, beyond, d_in, d1)
        return five_point(
            c, e, w, n, s,
            [north_of(x, x[15:16]) for x in c[:2]],
            [south_of(x, x[0:1]) for x in c[:2]],
            as_wet(lev16 < d0),
            [as_wet(lev16 < x) for x in (d_e, d_w, d_n, d_s)],
            as_wet(lev16 + 1.0 < d0),
            as_wet(jnp.logical_and(sub16 >= 1, lev16 - 1.0 < d0)),
            angles[64 + at : 65 + at, :],
            angles[66 + at : 67 + at, :],
        )

    south_mid = halo_row(south_rows, cols_s, corner_depth[0], 0, False, 0)
    north_mid = halo_row(north_rows, cols_n, corner_depth[1], ROWS - 1, True, 1)

    d_e = jnp.where(lane == 127, shift(col_depth, 125), shift(depth, -1))
    d_w = jnp.where(lane == 0, shift(col_depth, 123), shift(depth, 1))
    d_n = north_of(depth, north_rows[128:129])
    d_s = south_of(depth, south_rows[128:129])
    m_e, m_w, m_n, m_s = (jnp.minimum(depth, x) for x in (d_e, d_w, d_n, d_s))
    last_row = lax.broadcasted_iota(jnp.int32, (ROWS, LANES), 0) == ROWS - 1
    first_row = lax.broadcasted_iota(jnp.int32, (ROWS, LANES), 0) == 0

    def whole_step(read, col_values, rows_s, rows_n, write):
        sides = [jnp.where(place == 2, x, shift(x, -2)) for x in col_values]
        now = [read(f, 0) for f in range(4)]
        carried = [None, None]
        for k in range(LEVELS):
            above = [read(f, k + 1) for f in range(4)] if k + 1 < LEVELS else None
            half_e, half_w, half_n, half_s = (jnp.where(k < x, 0.5, 0.0) for x in (m_e, m_w, m_n, m_s))
            e, w, n, s = [], [], [], []
            for f in range(4):
                x = now[f]
                ends = shift(sides[f], 127 - (8 * k + 2))
                e.append(jnp.where(lane == 127, ends, shift(x, -1)))
                w.append(jnp.where(lane == 0, ends, shift(x, 1)))
                n.append(jnp.where(last_row, rows_n[f][k : k + 1], shift(x, -1, 0)))
                s.append(jnp.where(first_row, rows_s[f][k : k + 1], shift(x, 1, 0)))
            flow_e = (now[2] + e[2]) * half_e
            flow_w = (now[2] + w[2]) * half_w
            flow_n = (now[3] + n[3]) * half_n
            flow_s = (now[3] + s[3]) * half_s
            out_e, in_e = jnp.maximum(flow_e, 0.0), jnp.minimum(flow_e, 0.0)
            in_w, out_w = jnp.maximum(flow_w, 0.0), jnp.minimum(flow_w, 0.0)
            out_n, in_n = jnp.maximum(flow_n, 0.0), jnp.minimum(flow_n, 0.0)
            in_s, out_s = jnp.maximum(flow_s, 0.0), jnp.minimum(flow_s, 0.0)
            kept = 1.0 - ((out_e - out_w) + (out_n - out_s))
            wet = k < depth
            new = []
            for f in range(2):
                x = now[f]
                total = (x * kept - (in_e * e[f] - in_w * w[f])) - (in_n * n[f] - in_s * s[f])
                if above is not None:
                    flux = jnp.where(k + 1 < depth, MIXING * (above[f] - x), 0.0)
                    total = total + flux
                if carried[f] is not None:
                    total = total - carried[f]
                if above is not None:
                    carried[f] = flux
                new.append(jnp.where(wet, total, 0.0))
            thick = 2.0 * VISCOSITY
            vis_e, vis_w, vis_n, vis_s = (thick * x for x in (half_e, half_w, half_n, half_s))
            kept = kept - ((vis_e + vis_w) + (vis_n + vis_s))
            in_e, in_w, in_n, in_s = vis_e - in_e, vis_w + in_w, vis_n - in_n, vis_s + in_s
            ua, va = (
                (now[f] * kept + (in_e * e[f] + in_w * w[f])) + (in_n * n[f] + in_s * s[f]) for f in (2, 3)
            )
            new.append(jnp.where(wet, cosine * ua + sine * va, 0.0))
            new.append(jnp.where(wet, cosine * va - sine * ua, 0.0))
            for f in range(4):
                write(f, k, new[f])
            now = above

    def to_mid(f, k, value):
        mid[f, k] = value

    outs = (heat_out, salt_out, zonal_out, merid_out)

    def to_out(f, k, value):
        outs[f][k] = value

    whole_step(
        lambda f, k: fields[f][k],
        cols,
        [south_rows[f * 16 : f * 16 + 16] for f in range(4)],
        [north_rows[f * 16 : f * 16 + 16] for f in range(4)],
        to_mid,
    )
    whole_step(lambda f, k: mid[f, k], cols_mid, south_mid, north_mid, to_out)


def shapes(*dims):
    return [jax.ShapeDtypeStruct(d, jnp.float32) for d in dims]


def call(kernel, outputs, *operands, scratch=()):
    vmem = pl.BlockSpec(memory_space=pltpu.VMEM)
    return pl.pallas_call(
        kernel,
        out_shape=shapes(*outputs),
        in_specs=[vmem] * len(operands),
        out_specs=[vmem] * len(outputs),
        scratch_shapes=list(scratch),
        compiler_params=pltpu.CompilerParams(vmem_limit_bytes=32 * 1024 * 1024),
    )(*operands)


def angle_table():
    first = lax.axis_index("lat") * ROWS
    total = ROWS * N_LAT
    ids = jnp.concatenate([jnp.arange(ROWS), jnp.array([-1, ROWS])]) + first
    ids = jnp.where(ids >= total, 2 * total - 1 - ids, ids)
    angle = ROTATION * (2.0 * (ids.astype(jnp.float32) + 0.5) / total - 1.0)
    c, s = jnp.cos(angle), jnp.sin(angle)
    column = jnp.concatenate([c[:ROWS], s[:ROWS], c[ROWS:], s[ROWS:], jnp.zeros((4,), jnp.float32)])
    return jnp.broadcast_to(column[:, None], (72, LANES))


def on_device(heat, salt, zonal, merid, flag, tally):
    whole = (heat, salt, zonal, merid, flag, tally)
    row_even, row_odd, packed, col_near, col_far = call(
        pack_kernel,
        [(ROW_MSG, LANES), (ROW_MSG, LANES), (4, ROWS, LANES), (40, LANES), (40, LANES)],
        *whole,
    )
    everyone, edges = (lambda lat: True), is_edge
    corner = send(row_odd[128:136], near_corner_relay, edges)
    odd = send(row_odd, odd_or_diagonal, lambda lat: lat > 0)
    even = send(row_even, even_lat, everyone)
    to_near, to_far, to_far_edge = call(
        relay_kernel,
        [(COL_MSG, LANES), (COL_MSG, LANES), (EDGE_MSG, LANES)],
        even, odd, corner, col_near, col_far,
    )
    far_edge = send(to_far_edge, far_lon, edges)
    far = send(to_far, far_lon, lambda lat: not is_edge(lat))
    near = send(to_near, near_lon, everyone)
    size = (LEVELS, ROWS, LANES)
    return tuple(
        call(
            step_kernel,
            [size] * 4,
            *whole, packed, angle_table(), even, odd, near, far, far_edge,
            scratch=[pltpu.VMEM((4,) + size, jnp.float32)],
        )
    )


def solution(mesh):
    field, column = P(None, "lat", "lon"), P("lat", "lon")
    return jax.shard_map(
        on_device,
        mesh=mesh,
        in_specs=(field,) * 4 + (column,) * 2,
        out_specs=(field,) * 4,
        check_vma=False,
    )
```

```python
import jax
import jax.numpy as jnp
from jax import lax
from jax.experimental import pallas as pl
from jax.experimental.pallas import tpu as pltpu
from jax.sharding import PartitionSpec as P

MIXING = 0.2
VISCOSITY = 0.05
ROTATION = 0.3
LEVELS = 16
ROWS = 32
LANES = 128
N_LAT = 32
N_LON = 16
BLOCK = 8
ROW_MSG = 136
COL_MSG = 48
CHUNK = 4
EDGE_MSG = COL_MSG + ROW_MSG


def near_lon(lat, lon):
    return lat, lon ^ 1


def far_lon(lat, lon):
    return lat, (lon + 1) % N_LON if lon % 2 else (lon - 1) % N_LON


def even_lat(lat, lon):
    return lat ^ 1, lon


def odd_lat(lat, lon):
    if lat == N_LAT - 1:
        return lat, N_LON - 1 - lon
    return (lat + 1 if lat % 2 else lat - 1), lon


def is_edge(lat):
    return lat > 0 and lat % BLOCK in (0, BLOCK - 1)


def upper(lon):
    return lon // 2 % 2 == 1


def pairs(where_to, member):
    found = []
    for lat in range(N_LAT):
        for lon in range(N_LON):
            if member(lat, lon):
                to_lat, to_lon = where_to(lat, lon)
                found.append((lat * N_LON + lon, to_lat * N_LON + to_lon))
    return found


def send(array, where_to, member):
    return lax.ppermute(array, ("lat", "lon"), pairs(where_to, member))


def odd_or_diagonal(lat, lon):
    to = odd_lat(lat, lon)
    return far_lon(*to) if is_edge(lat) else to


def shift(x, by, axis=1):
    by = by % x.shape[axis]
    return x if by == 0 else pltpu.roll(x, by, axis)


def lanes_of(shape):
    return lax.broadcasted_iota(jnp.int32, shape, 1)


def position():
    return lax.axis_index("lat"), lax.axis_index("lon")


def is_upper(lon):
    return lax.rem(lax.div(lon, 2), 2) == 1


def pack_kernel(
    heat_in, salt_in, zonal_in, merid_in, flag_in, tally_in,
    row_even, row_odd, packed, col_near, col_far,
    heat, salt, zonal, merid, flag, tally, sems,
):
    copies = [
        pltpu.make_async_copy(source, held, sems.at[i])
        for i, (source, held) in enumerate(
            (
                (flag_in, flag), (tally_in, tally), (heat_in, heat),
                (salt_in, salt), (zonal_in, zonal), (merid_in, merid),
            )
        )
    ]
    for copy in copies:
        copy.start()
    lat, lon = position()
    lat_odd = lax.rem(lat, 2) == 1
    lon_odd = lax.rem(lon, 2) == 1
    copies[0].wait()
    copies[1].wait()
    depth = (flag[...] * tally[...]).astype(jnp.float32)
    lane = lanes_of((ROWS, LANES))
    group = lane >> 3
    pair = (lane & 7) >> 1
    west = jnp.zeros((ROWS, LANES), jnp.float32)
    east = west
    for f, field in enumerate((heat, salt, zonal, merid)):
        copies[2 + f].wait()
        acc = jnp.zeros((ROWS, LANES), jnp.float32)
        for k in range(LEVELS):
            acc = jnp.where(group == k, shift(field[k], 8 * k + 2), acc)
        packed[f] = acc
        west = jnp.where(pair == f, shift(acc, 2 * f - 2), west)
        east = jnp.where(pair == f, shift(acc, 2 * f), east)
        for d in range(2):
            at = (d * 4 + f) * LEVELS
            top = field[:, ROWS - 1 - d, :]
            bottom = field[:, d, :]
            row_even[at : at + LEVELS, :] = jnp.where(lat_odd, bottom, top)
            row_odd[at : at + LEVELS, :] = jnp.where(lat_odd, top, bottom)
    short = lanes_of((8, LANES)) >> 1
    depth_west = jnp.zeros((8, LANES), jnp.float32)
    depth_east = depth_west
    for i in range(4):
        part = depth[8 * i : 8 * i + 8]
        depth_west = jnp.where(short == i, shift(part, 2 * i), depth_west)
        depth_east = jnp.where(short == i, shift(part, 2 * i + 2), depth_east)
    col_near[0:ROWS, :] = jnp.where(lon_odd, west, east)
    col_far[0:ROWS, :] = jnp.where(lon_odd, east, west)
    col_near[ROWS : ROWS + 8, :] = jnp.where(lon_odd, depth_west, depth_east)
    col_far[ROWS : ROWS + 8, :] = jnp.where(lon_odd, depth_east, depth_west)
    blank = jnp.zeros((4, LANES), jnp.float32)
    tops = jnp.concatenate([depth[31:32], depth[30:31], west[31:32], east[31:32], blank], 0)
    bottoms = jnp.concatenate([depth[0:1], depth[1:2], west[0:1], east[0:1], blank], 0)
    row_even[128:136, :] = jnp.where(lat_odd, bottoms, tops)
    row_odd[128:136, :] = jnp.where(lat_odd, tops, bottoms)


def join_kernel(row_even, row_odd, near, low_out, odd_out, up_out):
    lat, _ = position()
    lat_odd = lax.rem(lat, 2) == 1
    blank = jnp.zeros((2, LANES), jnp.float32)
    top = jnp.concatenate([near[31:32, :], shift(near[39:40, :], -6), blank], 0)
    bottom = jnp.concatenate([near[0:1, :], near[32:33, :], blank], 0)
    low_out[0:132, :] = row_even[0:132, :]
    up_out[0:132, :] = row_even[0:132, :]
    odd_out[0:132, :] = row_odd[0:132, :]
    low_out[132:136, :] = jnp.where(lat_odd, bottom, top)
    up_out[132:136, :] = jnp.where(lat_odd, bottom, top)
    odd_out[132:136, :] = jnp.where(lat_odd, top, bottom)


def relay_kernel(even_low, odd, even_up, col_far, to_far, to_far_edge):
    _, lon = position()
    lon_odd = lax.rem(lon, 2) == 1
    info_even = jnp.where(is_upper(lon), even_up[128:136, :], even_low[128:136, :])
    info_odd = odd[128:136, :]
    blank = jnp.zeros((4, LANES), jnp.float32)

    def corners(row):
        return jnp.concatenate(
            [info_even[row : row + 1], info_odd[row : row + 1], info_even[0:1], info_odd[0:1], blank], 0
        )

    far_tile = jnp.where(lon_odd, corners(3), corners(2))
    to_far[0:40, :] = col_far[...]
    to_far[40:48, :] = far_tile
    to_far_edge[0:40, :] = col_far[...]
    to_far_edge[40:48, :] = far_tile
    to_far_edge[48:184, :] = odd[...]


def reversed_lanes(x):
    lane = lanes_of(x.shape)
    for b in range(7):
        x = jnp.where((lane >> b) & 1 == 1, shift(x, 1 << b), shift(x, -(1 << b)))
    return x


def five_point(c, e, w, n, s, up, down, wet, wets, wet_up, wet_down, cosine, sine):
    wet_e, wet_w, wet_n, wet_s = (wet * x for x in wets)
    flow_e = 0.5 * (c[2] + e[2]) * wet_e
    flow_w = 0.5 * (c[2] + w[2]) * wet_w
    flow_n = 0.5 * (c[3] + n[3]) * wet_n
    flow_s = 0.5 * (c[3] + s[3]) * wet_s

    def gain(f, viscosity):
        east = (jnp.maximum(flow_e, 0.0) * c[f] + jnp.minimum(flow_e, 0.0) * e[f]) - viscosity * wet_e * (e[f] - c[f])
        west = (jnp.maximum(flow_w, 0.0) * w[f] + jnp.minimum(flow_w, 0.0) * c[f]) - viscosity * wet_w * (c[f] - w[f])
        north = (jnp.maximum(flow_n, 0.0) * c[f] + jnp.minimum(flow_n, 0.0) * n[f]) - viscosity * wet_n * (n[f] - c[f])
        south = (jnp.maximum(flow_s, 0.0) * s[f] + jnp.minimum(flow_s, 0.0) * c[f]) - viscosity * wet_s * (c[f] - s[f])
        return c[f] - ((east - west) + (north - south))

    def tracer(f):
        mixed = MIXING * ((up[f] - c[f]) * (wet * wet_up) - (c[f] - down[f]) * (wet * wet_down))
        return wet * (gain(f, 0.0) + mixed)

    ua, va = gain(2, VISCOSITY), gain(3, VISCOSITY)
    return [tracer(0), tracer(1), wet * (cosine * ua + sine * va), wet * (cosine * va - sine * ua)]


def north_of(x, last):
    return jnp.concatenate([x[1:], last], 0)


def south_of(x, first):
    return jnp.concatenate([first, x[:-1]], 0)


def as_wet(mask):
    return jnp.where(mask, 1.0, 0.0)


def step_kernel(
    heat, salt, zonal, merid, flag, tally, packed, angles, even_low, odd, even_up, near, far, far_edge,
    heat_out, salt_out, zonal_out, merid_out, mid, last, sems,
):
    lat, lon = position()
    lat_odd = lax.rem(lat, 2) == 1
    lon_odd = lax.rem(lon, 2) == 1
    at_top = lat == N_LAT - 1
    run = lax.rem(lat, BLOCK)
    edge = jnp.logical_and(lat > 0, jnp.logical_or(run == 0, run == BLOCK - 1))
    fields = (heat, salt, zonal, merid)
    lane = lanes_of((ROWS, LANES))
    place = lane & 7
    level = (lane >> 3).astype(jnp.float32)
    lane1 = lanes_of((1, LANES))
    place1 = lane1 & 7
    depth = (flag[...] * tally[...]).astype(jnp.float32)
    cosine, sine = angles[0:32, :], angles[32:64, :]

    signs = jnp.where(jnp.logical_and(at_top, place1 >= 4), -1.0, 1.0)

    def swap_pair(x):
        return jnp.where(lane1 & 1 == 1, shift(x, 1), shift(x, -1)) * signs

    odd_rows = jnp.where(edge, far_edge[48:184, :], odd[...])
    beside = odd_rows[132:134]
    turned = reversed_lanes(odd_rows)
    row_field = (lax.broadcasted_iota(jnp.int32, (ROW_MSG, LANES), 0) >> 4) & 3
    below = lax.broadcasted_iota(jnp.int32, (ROW_MSG, LANES), 0) < 128
    turned = jnp.where(jnp.logical_and(below, row_field >= 2), -turned, turned)
    odd_rows = jnp.where(at_top, turned, odd_rows)
    even_rows = jnp.where(is_upper(lon), even_up[...], even_low[...])
    south_rows = jnp.where(lat_odd, even_rows, odd_rows)
    north_rows = jnp.where(lat_odd, odd_rows, even_rows)
    far_cols = jnp.where(edge, far_edge[0:48, :], far[...])
    near_cols = near[...]
    west_cols = jnp.where(lon_odd, near_cols, far_cols[0:40])
    east_cols = jnp.where(lon_odd, far_cols[0:40], near_cols)

    q = odd[128:136, :]
    q_west = jnp.where(at_top, swap_pair(q[3:4]), q[2:3])
    q_east = jnp.where(at_top, swap_pair(q[2:3]), q[3:4])
    q_depth = jnp.where(at_top, reversed_lanes(q[0:1]), q[0:1])
    far_even = far_cols[40:41]
    far_odd = jnp.where(edge, jnp.where(lon_odd, q_west, q_east), far_cols[41:42])
    far_odd_d = jnp.where(edge, q_depth, far_cols[43:44])
    near_even, near_even_d = even_rows[132:133], even_rows[133:134]
    near_odd = jnp.where(at_top, swap_pair(beside[0:1]), beside[0:1])
    near_odd_d = jnp.where(at_top, jnp.where(lane1 == 0, shift(beside[1:2], -1), shift(beside[1:2], 1)), beside[1:2])

    def near_depth(row):
        return jnp.where(lon_odd, row[:, 1:2], row[:, 0:1])

    def far_depth(row):
        return jnp.where(lon_odd, row[:, 0:1], row[:, 127:128])

    def by_side(even_part, odd_part):
        return jnp.where(lat_odd, even_part, odd_part), jnp.where(lat_odd, odd_part, even_part)

    def west_east(near_part, far_part):
        return jnp.where(lon_odd, near_part, far_part), jnp.where(lon_odd, far_part, near_part)

    near_s, near_n = by_side(near_even, near_odd)
    far_s, far_n = by_side(far_even, far_odd)
    (sw, se), (nw, ne) = west_east(near_s, far_s), west_east(near_n, far_n)
    near_sd, near_nd = by_side(near_depth(near_even_d), near_depth(near_odd_d))
    far_sd, far_nd = by_side(far_depth(far_cols[42:43]), far_depth(far_odd_d))
    corner_depth = [west_east(near_sd, far_sd), west_east(near_nd, far_nd)]

    cols, cols_s, cols_n = [], [], []
    for f in range(4):
        own = packed[f]
        x = jnp.where(place < 2, own, shift(own, 4))
        x = jnp.where((place >> 1) == 1, shift(east_cols[0:32], 2 - 2 * f), x)
        x = jnp.where((place >> 1) == 2, shift(west_cols[0:32], 4 - 2 * f), x)
        cols.append(x)
        for out, w, e in ((cols_s, sw, se), (cols_n, nw, ne)):
            out.append(
                jnp.where(place1 == 5, shift(w, 4 - 2 * f), jnp.where(place1 == 2, shift(e, 2 - 2 * f), 0.0))
            )
    west_d = jnp.concatenate([shift(west_cols[32:40], 4 - 2 * i) for i in range(4)], 0)
    east_d = jnp.concatenate([shift(east_cols[32:40], 2 - 2 * i) for i in range(4)], 0)
    col_depth = jnp.where(lane < 2, shift(depth, 2), shift(depth, 6))
    col_depth = jnp.where((lane >> 1) == 1, east_d, col_depth)
    col_depth = jnp.where((lane >> 1) == 2, west_d, col_depth)
    col_depth = jnp.where(lane < 8, col_depth, 0.0)
    for b in (8, 16, 32, 64):
        col_depth = col_depth + shift(col_depth, b)
    corner_rows = [
        jnp.where(place1 == 5, w, jnp.where(place1 == 2, e, 0.0)) for w, e in corner_depth
    ]

    wets = [
        as_wet(level < x)
        for x in (
            shift(col_depth, -1),
            shift(col_depth, 1),
            north_of(col_depth, corner_rows[1]),
            south_of(col_depth, corner_rows[0]),
        )
    ]
    cols_mid = five_point(
        cols,
        [shift(x, -1) for x in cols],
        [shift(x, 1) for x in cols],
        [north_of(x, y) for x, y in zip(cols, cols_n)],
        [south_of(x, y) for x, y in zip(cols, cols_s)],
        [shift(x, -8) for x in cols[:2]],
        [shift(x, 8) for x in cols[:2]],
        as_wet(level < col_depth),
        wets,
        as_wet(level + 1.0 < col_depth),
        as_wet(jnp.logical_and(lane >= 8, level - 1.0 < col_depth)),
        cosine,
        sine,
    )

    lane16 = lanes_of((LEVELS, LANES))
    sub16 = lax.broadcasted_iota(jnp.int32, (LEVELS, LANES), 0)
    lev16 = sub16.astype(jnp.float32)

    def halo_row(rows, corner_cols, corner_d, own_row, north, at):
        c = [rows[f * 16 : f * 16 + 16] for f in range(4)]
        beyond = [rows[64 + f * 16 : 64 + f * 16 + 16] for f in range(4)]
        inner = [x[:, own_row, :] for x in fields]
        d0, d1, d_in = rows[128:129], rows[129:130], depth[own_row : own_row + 1]
        d_w = jnp.where(lane1 == 0, corner_d[0], shift(d0, 1))
        d_e = jnp.where(lane1 == 127, corner_d[1], shift(d0, -1))
        e, w = [], []
        for f in range(4):
            spread_out = jnp.broadcast_to(corner_cols[f], (LEVELS, LANES))
            at_w = jnp.sum(jnp.where(lane16 == 8 * sub16 + 5, spread_out, 0.0), axis=1, keepdims=True)
            at_e = jnp.sum(jnp.where(lane16 == 8 * sub16 + 2, spread_out, 0.0), axis=1, keepdims=True)
            w.append(jnp.where(lane16 == 0, at_w, shift(c[f], 1)))
            e.append(jnp.where(lane16 == 127, at_e, shift(c[f], -1)))
        n, s, d_n, d_s = (beyond, inner, d1, d_in) if north else (inner, beyond, d_in, d1)
        return five_point(
            c, e, w, n, s,
            [north_of(x, x[15:16]) for x in c[:2]],
            [south_of(x, x[0:1]) for x in c[:2]],
            as_wet(lev16 < d0),
            [as_wet(lev16 < x) for x in (d_e, d_w, d_n, d_s)],
            as_wet(lev16 + 1.0 < d0),
            as_wet(jnp.logical_and(sub16 >= 1, lev16 - 1.0 < d0)),
            angles[64 + at : 65 + at, :],
            angles[66 + at : 67 + at, :],
        )

    south_mid = halo_row(south_rows, cols_s, corner_depth[0], 0, False, 0)
    north_mid = halo_row(north_rows, cols_n, corner_depth[1], ROWS - 1, True, 1)

    d_e = jnp.where(lane == 127, shift(col_depth, 125), shift(depth, -1))
    d_w = jnp.where(lane == 0, shift(col_depth, 123), shift(depth, 1))
    d_n = north_of(depth, north_rows[128:129])
    d_s = south_of(depth, south_rows[128:129])
    m_e, m_w, m_n, m_s = (jnp.minimum(depth, x) for x in (d_e, d_w, d_n, d_s))
    last_row = lax.broadcasted_iota(jnp.int32, (ROWS, LANES), 0) == ROWS - 1
    first_row = lax.broadcasted_iota(jnp.int32, (ROWS, LANES), 0) == 0

    def whole_step(read, col_values, rows_s, rows_n, write):
        sides = [jnp.where(place == 2, x, shift(x, -2)) for x in col_values]
        now = [read(f, 0) for f in range(4)]
        carried = [None, None]
        for k in range(LEVELS):
            above = [read(f, k + 1) for f in range(4)] if k + 1 < LEVELS else None
            half_e, half_w, half_n, half_s = (jnp.where(k < x, 0.5, 0.0) for x in (m_e, m_w, m_n, m_s))
            e, w, n, s = [], [], [], []
            for f in range(4):
                x = now[f]
                ends = shift(sides[f], 127 - (8 * k + 2))
                e.append(jnp.where(lane == 127, ends, shift(x, -1)))
                w.append(jnp.where(lane == 0, ends, shift(x, 1)))
                n.append(jnp.where(last_row, rows_n[f][k : k + 1], shift(x, -1, 0)))
                s.append(jnp.where(first_row, rows_s[f][k : k + 1], shift(x, 1, 0)))
            flow_e = (now[2] + e[2]) * half_e
            flow_w = (now[2] + w[2]) * half_w
            flow_n = (now[3] + n[3]) * half_n
            flow_s = (now[3] + s[3]) * half_s
            out_e, in_e = jnp.maximum(flow_e, 0.0), jnp.minimum(flow_e, 0.0)
            in_w, out_w = jnp.maximum(flow_w, 0.0), jnp.minimum(flow_w, 0.0)
            out_n, in_n = jnp.maximum(flow_n, 0.0), jnp.minimum(flow_n, 0.0)
            in_s, out_s = jnp.maximum(flow_s, 0.0), jnp.minimum(flow_s, 0.0)
            kept = 1.0 - ((out_e - out_w) + (out_n - out_s))
            wet = k < depth
            new = []
            for f in range(2):
                x = now[f]
                total = (x * kept - (in_e * e[f] - in_w * w[f])) - (in_n * n[f] - in_s * s[f])
                if above is not None:
                    flux = jnp.where(k + 1 < depth, MIXING * (above[f] - x), 0.0)
                    total = total + flux
                if carried[f] is not None:
                    total = total - carried[f]
                if above is not None:
                    carried[f] = flux
                new.append(jnp.where(wet, total, 0.0))
            thick = 2.0 * VISCOSITY
            vis_e, vis_w, vis_n, vis_s = (thick * x for x in (half_e, half_w, half_n, half_s))
            kept = kept - ((vis_e + vis_w) + (vis_n + vis_s))
            in_e, in_w, in_n, in_s = vis_e - in_e, vis_w + in_w, vis_n - in_n, vis_s + in_s
            ua, va = (
                (now[f] * kept + (in_e * e[f] + in_w * w[f])) + (in_n * n[f] + in_s * s[f]) for f in (2, 3)
            )
            new.append(jnp.where(wet, cosine * ua + sine * va, 0.0))
            new.append(jnp.where(wet, cosine * va - sine * ua, 0.0))
            for f in range(4):
                write(f, k, new[f])
            now = above

    def to_mid(f, k, value):
        mid[f, k] = value

    outs = (heat_out, salt_out, zonal_out, merid_out)

    copies = []

    def to_out(f, k, value):
        last[f, k] = value
        if k % CHUNK == CHUNK - 1:
            part = pl.ds(k + 1 - CHUNK, CHUNK)
            copy = pltpu.make_async_copy(last.at[f, part], outs[f].at[part], sems.at[f, k // CHUNK])
            copy.start()
            copies.append(copy)

    whole_step(
        lambda f, k: fields[f][k],
        cols,
        [south_rows[f * 16 : f * 16 + 16] for f in range(4)],
        [north_rows[f * 16 : f * 16 + 16] for f in range(4)],
        to_mid,
    )
    whole_step(lambda f, k: mid[f, k], cols_mid, south_mid, north_mid, to_out)
    for copy in copies:
        copy.wait()


def shapes(*dims):
    return [jax.ShapeDtypeStruct(d, jnp.float32) for d in dims]


def call(kernel, outputs, *operands, scratch=(), held_in=True, held_out=True, grant=32):
    vmem, hbm = pl.BlockSpec(memory_space=pltpu.VMEM), pl.BlockSpec(memory_space=pltpu.HBM)
    return pl.pallas_call(
        kernel,
        out_shape=shapes(*outputs),
        in_specs=[vmem if held_in else hbm] * len(operands),
        out_specs=[vmem if held_out else hbm] * len(outputs),
        scratch_shapes=list(scratch),
        compiler_params=pltpu.CompilerParams(vmem_limit_bytes=int(grant * 1024 * 1024)),
    )(*operands)


def angle_table():
    first = lax.axis_index("lat") * ROWS
    total = ROWS * N_LAT
    ids = jnp.concatenate([jnp.arange(ROWS), jnp.array([-1, ROWS])]) + first
    ids = jnp.where(ids >= total, 2 * total - 1 - ids, ids)
    angle = ROTATION * (2.0 * (ids.astype(jnp.float32) + 0.5) / total - 1.0)
    c, s = jnp.cos(angle), jnp.sin(angle)
    column = jnp.concatenate([c[:ROWS], s[:ROWS], c[ROWS:], s[ROWS:], jnp.zeros((4,), jnp.float32)])
    return jnp.broadcast_to(column[:, None], (72, LANES))


def on_device(heat, salt, zonal, merid, flag, tally):
    whole = (heat, salt, zonal, merid, flag, tally)
    size = (LEVELS, ROWS, LANES)
    pinned = [pltpu.with_memory_space_constraint(x, pltpu.HBM) for x in whole]
    row_even, row_odd, packed, col_near, col_far = call(
        pack_kernel,
        [(ROW_MSG, LANES), (ROW_MSG, LANES), (4, ROWS, LANES), (40, LANES), (40, LANES)],
        *pinned,
        scratch=[pltpu.VMEM(size, jnp.float32)] * 4
        + [pltpu.VMEM((ROWS, LANES), jnp.int32)] * 2
        + [pltpu.SemaphoreType.DMA((6,))],
        held_in=False,
    )
    near = send(col_near, near_lon, lambda lat, lon: True)
    row_low, row_odd, row_up = call(join_kernel, [(ROW_MSG, LANES)] * 3, row_even, row_odd, near)
    even_low = send(row_low, even_lat, lambda lat, lon: not upper(lon))
    odd = send(row_odd, odd_or_diagonal, lambda lat, lon: lat > 0)
    even_up = send(row_up, even_lat, lambda lat, lon: upper(lon))
    to_far, to_far_edge = call(
        relay_kernel, [(COL_MSG, LANES), (EDGE_MSG, LANES)], even_low, odd, even_up, col_far
    )
    far = send(to_far, far_lon, lambda lat, lon: not is_edge(lat))
    far_edge = send(to_far_edge, far_lon, lambda lat, lon: is_edge(lat))
    return tuple(
        call(
            step_kernel,
            [size] * 4,
            *whole, packed, angle_table(), even_low, odd, even_up, near, far, far_edge,
            scratch=[
                pltpu.VMEM((4,) + size, jnp.float32),
                pltpu.VMEM((4,) + size, jnp.float32),
                pltpu.SemaphoreType.DMA((4, LEVELS // CHUNK)),
            ],
            held_out=False,
        )
    )


def solution(mesh):
    field, column = P(None, "lat", "lon"), P("lat", "lon")
    return jax.shard_map(
        on_device,
        mesh=mesh,
        in_specs=(field,) * 4 + (column,) * 2,
        out_specs=(field,) * 4,
        check_vma=False,
    )
```

```python
import jax
import jax.numpy as jnp
from jax import lax
from jax.experimental import pallas as pl
from jax.experimental.pallas import tpu as pltpu
from jax.sharding import PartitionSpec as P

MIXING = 0.2
VISCOSITY = 0.05
ROTATION = 0.3
LEVELS = 16
ROWS = 32
LANES = 128
N_LAT = 32
N_LON = 16
BLOCK = 8
ROW_MSG = 136
COL_MSG = 48
CHUNK = 4
EDGE_MSG = COL_MSG + ROW_MSG


def near_lon(lat, lon):
    return lat, lon ^ 1


def far_lon(lat, lon):
    return lat, (lon + 1) % N_LON if lon % 2 else (lon - 1) % N_LON


def even_lat(lat, lon):
    return lat ^ 1, lon


def odd_lat(lat, lon):
    if lat == N_LAT - 1:
        return lat, N_LON - 1 - lon
    return (lat + 1 if lat % 2 else lat - 1), lon


def is_edge(lat):
    return lat > 0 and lat % BLOCK in (0, BLOCK - 1)


def upper(lon):
    return lon // 2 % 2 == 1


def pairs(where_to, member):
    found = []
    for lat in range(N_LAT):
        for lon in range(N_LON):
            if member(lat, lon):
                to_lat, to_lon = where_to(lat, lon)
                found.append((lat * N_LON + lon, to_lat * N_LON + to_lon))
    return found


def send(array, where_to, member):
    return lax.ppermute(array, ("lat", "lon"), pairs(where_to, member))


def odd_or_diagonal(lat, lon):
    to = odd_lat(lat, lon)
    return far_lon(*to) if is_edge(lat) else to


def shift(x, by, axis=1):
    by = by % x.shape[axis]
    return x if by == 0 else pltpu.roll(x, by, axis)


def lanes_of(shape):
    return lax.broadcasted_iota(jnp.int32, shape, 1)


def position():
    return lax.axis_index("lat"), lax.axis_index("lon")


def is_upper(lon):
    return lax.rem(lax.div(lon, 2), 2) == 1


def pack_kernel(
    heat_in, salt_in, zonal_in, merid_in, flag_in, tally_in,
    heat, salt, zonal, merid, depth_out, packed, info_top, info_bottom, col_near, col_far,
    flag, tally, sems,
):
    copies = [
        pltpu.make_async_copy(source, held, sems.at[i])
        for i, (source, held) in enumerate(
            (
                (flag_in, flag), (tally_in, tally), (heat_in, heat),
                (salt_in, salt), (zonal_in, zonal), (merid_in, merid),
            )
        )
    ]
    for copy in copies:
        copy.start()
    _, lon = position()
    lon_odd = lax.rem(lon, 2) == 1
    copies[0].wait()
    copies[1].wait()
    depth = (flag[...] * tally[...]).astype(jnp.float32)
    depth_out[...] = depth
    lane = lanes_of((ROWS, LANES))
    group = lane >> 3
    pair = (lane & 7) >> 1
    west = jnp.zeros((ROWS, LANES), jnp.float32)
    east = west
    for f, field in enumerate((heat, salt, zonal, merid)):
        copies[2 + f].wait()
        acc = jnp.zeros((ROWS, LANES), jnp.float32)
        for k in range(LEVELS):
            acc = jnp.where(group == k, shift(field[k], 8 * k + 2), acc)
        packed[f] = acc
        west = jnp.where(pair == f, shift(acc, 2 * f - 2), west)
        east = jnp.where(pair == f, shift(acc, 2 * f), east)
    short = lanes_of((8, LANES)) >> 1
    depth_west = jnp.zeros((8, LANES), jnp.float32)
    depth_east = depth_west
    for i in range(4):
        part = depth[8 * i : 8 * i + 8]
        depth_west = jnp.where(short == i, shift(part, 2 * i), depth_west)
        depth_east = jnp.where(short == i, shift(part, 2 * i + 2), depth_east)
    col_near[0:ROWS, :] = jnp.where(lon_odd, west, east)
    col_far[0:ROWS, :] = jnp.where(lon_odd, east, west)
    col_near[ROWS : ROWS + 8, :] = jnp.where(lon_odd, depth_west, depth_east)
    col_far[ROWS : ROWS + 8, :] = jnp.where(lon_odd, depth_east, depth_west)
    blank = jnp.zeros((4, LANES), jnp.float32)
    info_top[...] = jnp.concatenate([depth[31:32], depth[30:31], west[31:32], east[31:32], blank], 0)
    info_bottom[...] = jnp.concatenate([depth[0:1], depth[1:2], west[0:1], east[0:1], blank], 0)


def row_kernel(heat, salt, zonal, merid, low_out, odd_out, up_out):
    lat, _ = position()
    lat_odd = lax.rem(lat, 2) == 1
    for f, field in enumerate((heat, salt, zonal, merid)):
        for d in range(2):
            at = (d * 4 + f) * LEVELS
            top = field[:, ROWS - 1 - d, :]
            bottom = field[:, d, :]
            even = jnp.where(lat_odd, bottom, top)
            low_out[at : at + LEVELS, :] = even
            up_out[at : at + LEVELS, :] = even
            odd_out[at : at + LEVELS, :] = jnp.where(lat_odd, top, bottom)


def join_kernel(low, odd, up, info_top, info_bottom, near, low_out, odd_out, up_out):
    lat, _ = position()
    lat_odd = lax.rem(lat, 2) == 1
    blank = jnp.zeros((2, LANES), jnp.float32)
    top = jnp.concatenate([info_top[0:4, :], near[31:32, :], shift(near[39:40, :], -6), blank], 0)
    bottom = jnp.concatenate([info_bottom[0:4, :], near[0:1, :], near[32:33, :], blank], 0)
    low_out[0:128, :] = low[...]
    up_out[0:128, :] = up[...]
    odd_out[0:128, :] = odd[...]
    even_info = jnp.where(lat_odd, bottom, top)
    low_out[128:136, :] = even_info
    up_out[128:136, :] = even_info
    odd_out[128:136, :] = jnp.where(lat_odd, top, bottom)


def relay_kernel(even_low, odd, even_up, col_far, to_far, to_far_edge):
    _, lon = position()
    lon_odd = lax.rem(lon, 2) == 1
    info_even = jnp.where(is_upper(lon), even_up[128:136, :], even_low[128:136, :])
    info_odd = odd[128:136, :]
    blank = jnp.zeros((4, LANES), jnp.float32)

    def corners(row):
        return jnp.concatenate(
            [info_even[row : row + 1], info_odd[row : row + 1], info_even[0:1], info_odd[0:1], blank], 0
        )

    far_tile = jnp.where(lon_odd, corners(3), corners(2))
    to_far[0:40, :] = col_far[...]
    to_far[40:48, :] = far_tile
    to_far_edge[0:40, :] = col_far[...]
    to_far_edge[40:48, :] = far_tile
    to_far_edge[48:184, :] = odd[...]


def reversed_lanes(x):
    lane = lanes_of(x.shape)
    for b in range(7):
        x = jnp.where((lane >> b) & 1 == 1, shift(x, 1 << b), shift(x, -(1 << b)))
    return x


def five_point(c, e, w, n, s, up, down, wet, wets, wet_up, wet_down, cosine, sine):
    wet_e, wet_w, wet_n, wet_s = (wet * x for x in wets)
    flow_e = 0.5 * (c[2] + e[2]) * wet_e
    flow_w = 0.5 * (c[2] + w[2]) * wet_w
    flow_n = 0.5 * (c[3] + n[3]) * wet_n
    flow_s = 0.5 * (c[3] + s[3]) * wet_s

    def gain(f, viscosity):
        east = (jnp.maximum(flow_e, 0.0) * c[f] + jnp.minimum(flow_e, 0.0) * e[f]) - viscosity * wet_e * (e[f] - c[f])
        west = (jnp.maximum(flow_w, 0.0) * w[f] + jnp.minimum(flow_w, 0.0) * c[f]) - viscosity * wet_w * (c[f] - w[f])
        north = (jnp.maximum(flow_n, 0.0) * c[f] + jnp.minimum(flow_n, 0.0) * n[f]) - viscosity * wet_n * (n[f] - c[f])
        south = (jnp.maximum(flow_s, 0.0) * s[f] + jnp.minimum(flow_s, 0.0) * c[f]) - viscosity * wet_s * (c[f] - s[f])
        return c[f] - ((east - west) + (north - south))

    def tracer(f):
        mixed = MIXING * ((up[f] - c[f]) * (wet * wet_up) - (c[f] - down[f]) * (wet * wet_down))
        return wet * (gain(f, 0.0) + mixed)

    ua, va = gain(2, VISCOSITY), gain(3, VISCOSITY)
    return [tracer(0), tracer(1), wet * (cosine * ua + sine * va), wet * (cosine * va - sine * ua)]


def north_of(x, last):
    return jnp.concatenate([x[1:], last], 0)


def south_of(x, first):
    return jnp.concatenate([first, x[:-1]], 0)


def as_wet(mask):
    return jnp.where(mask, 1.0, 0.0)


def column_groups(packed, depth, west_cols, east_cols):
    lane = lanes_of((ROWS, LANES))
    place = lane & 7
    cols = []
    for f in range(4):
        own = packed[f]
        x = jnp.where(place < 2, own, shift(own, 4))
        x = jnp.where((place >> 1) == 1, shift(east_cols[0:32], 2 - 2 * f), x)
        cols.append(jnp.where((place >> 1) == 2, shift(west_cols[0:32], 4 - 2 * f), x))
    west_d = jnp.concatenate([shift(west_cols[32:40], 4 - 2 * i) for i in range(4)], 0)
    east_d = jnp.concatenate([shift(east_cols[32:40], 2 - 2 * i) for i in range(4)], 0)
    col_depth = jnp.where(lane < 2, shift(depth, 2), shift(depth, 6))
    col_depth = jnp.where((lane >> 1) == 1, east_d, col_depth)
    col_depth = jnp.where((lane >> 1) == 2, west_d, col_depth)
    col_depth = jnp.where(lane < 8, col_depth, 0.0)
    for b in (8, 16, 32, 64):
        col_depth = col_depth + shift(col_depth, b)
    return cols, col_depth


def depths_beside(depth, col_depth, south, north):
    lane = lanes_of((ROWS, LANES))
    return (
        jnp.where(lane == 127, shift(col_depth, 125), shift(depth, -1)),
        jnp.where(lane == 0, shift(col_depth, 123), shift(depth, 1)),
        north_of(depth, north),
        south_of(depth, south),
    )


def whole_step(read, col_values, rows_s, rows_n, write, depth, beside, cosine, sine):
    lane = lanes_of((ROWS, LANES))
    place = lane & 7
    row = lax.broadcasted_iota(jnp.int32, (ROWS, LANES), 0)
    first_row, last_row = row == 0, row == ROWS - 1
    m_e, m_w, m_n, m_s = (jnp.minimum(depth, x) for x in beside)
    sides = [jnp.where(place == 2, x, shift(x, -2)) for x in col_values]
    now = [read(f, 0) for f in range(4)]
    carried = [None, None]
    for k in range(LEVELS):
        above = [read(f, k + 1) for f in range(4)] if k + 1 < LEVELS else None
        half_e, half_w, half_n, half_s = (jnp.where(k < x, 0.5, 0.0) for x in (m_e, m_w, m_n, m_s))
        e, w, n, s = [], [], [], []
        for f in range(4):
            x = now[f]
            ends = shift(sides[f], 127 - (8 * k + 2))
            e.append(jnp.where(lane == 127, ends, shift(x, -1)))
            w.append(jnp.where(lane == 0, ends, shift(x, 1)))
            n.append(jnp.where(last_row, rows_n[f][k : k + 1], shift(x, -1, 0)))
            s.append(jnp.where(first_row, rows_s[f][k : k + 1], shift(x, 1, 0)))
        flow_e = (now[2] + e[2]) * half_e
        flow_w = (now[2] + w[2]) * half_w
        flow_n = (now[3] + n[3]) * half_n
        flow_s = (now[3] + s[3]) * half_s
        out_e, in_e = jnp.maximum(flow_e, 0.0), jnp.minimum(flow_e, 0.0)
        in_w, out_w = jnp.maximum(flow_w, 0.0), jnp.minimum(flow_w, 0.0)
        out_n, in_n = jnp.maximum(flow_n, 0.0), jnp.minimum(flow_n, 0.0)
        in_s, out_s = jnp.maximum(flow_s, 0.0), jnp.minimum(flow_s, 0.0)
        kept = 1.0 - ((out_e - out_w) + (out_n - out_s))
        wet = k < depth
        new = []
        for f in range(2):
            x = now[f]
            total = (x * kept - (in_e * e[f] - in_w * w[f])) - (in_n * n[f] - in_s * s[f])
            if above is not None:
                flux = jnp.where(k + 1 < depth, MIXING * (above[f] - x), 0.0)
                total = total + flux
            if carried[f] is not None:
                total = total - carried[f]
            if above is not None:
                carried[f] = flux
            new.append(jnp.where(wet, total, 0.0))
        thick = 2.0 * VISCOSITY
        vis_e, vis_w, vis_n, vis_s = (thick * x for x in (half_e, half_w, half_n, half_s))
        kept = kept - ((vis_e + vis_w) + (vis_n + vis_s))
        in_e, in_w, in_n, in_s = vis_e - in_e, vis_w + in_w, vis_n - in_n, vis_s + in_s
        ua, va = (
            (now[f] * kept + (in_e * e[f] + in_w * w[f])) + (in_n * n[f] + in_s * s[f]) for f in (2, 3)
        )
        new.append(jnp.where(wet, cosine * ua + sine * va, 0.0))
        new.append(jnp.where(wet, cosine * va - sine * ua, 0.0))
        for f in range(4):
            write(f, k, new[f])
        now = above


def early_kernel(
    heat, salt, zonal, merid, depth_in, packed, angles, even_low, odd, even_up, near, mid_out
):
    lat, lon = position()
    lat_odd = lax.rem(lat, 2) == 1
    lon_odd = lax.rem(lon, 2) == 1
    fields = (heat, salt, zonal, merid)
    depth = depth_in[...]
    even_rows = jnp.where(is_upper(lon), even_up[...], even_low[...])
    odd_rows = odd[...]
    south_rows = jnp.where(lat_odd, even_rows, odd_rows)
    north_rows = jnp.where(lat_odd, odd_rows, even_rows)
    near_cols = near[...]
    west_cols = jnp.where(lon_odd, near_cols, 0.0)
    east_cols = jnp.where(lon_odd, 0.0, near_cols)
    cols, col_depth = column_groups(packed, depth, west_cols, east_cols)

    def write(f, k, value):
        mid_out[f, k] = value

    whole_step(
        lambda f, k: fields[f][k],
        cols,
        [south_rows[f * 16 : f * 16 + 16] for f in range(4)],
        [north_rows[f * 16 : f * 16 + 16] for f in range(4)],
        write,
        depth,
        depths_beside(depth, col_depth, south_rows[128:129], north_rows[128:129]),
        angles[0:32, :],
        angles[32:64, :],
    )


def step_kernel(
    mid, heat, salt, zonal, merid, depth_in, packed, angles, even_low, odd, even_up, near, far_edge, far,
    heat_out, salt_out, zonal_out, merid_out, turned, last, sems,
):
    lat, lon = position()
    lat_odd = lax.rem(lat, 2) == 1
    lon_odd = lax.rem(lon, 2) == 1
    at_top = lat == N_LAT - 1
    run = lax.rem(lat, BLOCK)
    edge = jnp.logical_and(lat > 0, jnp.logical_or(run == 0, run == BLOCK - 1))
    fields = (heat, salt, zonal, merid)
    lane = lanes_of((ROWS, LANES))
    place = lane & 7
    level = (lane >> 3).astype(jnp.float32)
    lane1 = lanes_of((1, LANES))
    place1 = lane1 & 7
    depth = depth_in[...]
    cosine, sine = angles[0:32, :], angles[32:64, :]

    signs = jnp.where(jnp.logical_and(at_top, place1 >= 4), -1.0, 1.0)

    def swap_pair(x):
        return jnp.where(lane1 & 1 == 1, shift(x, 1), shift(x, -1)) * signs

    odd_rows = jnp.where(edge, far_edge[48:184, :], odd[...])
    beside = odd_rows[132:134]
    turned[...] = odd_rows

    @pl.when(at_top)
    def _():
        for at in range(0, 130, 16):
            part = reversed_lanes(odd_rows[at : min(at + 16, 130)])
            turned[at : min(at + 16, 130), :] = -part if at < 128 and at // 16 % 4 >= 2 else part

    odd_info = odd_rows[130:132]
    odd_rows = turned[...]
    even_rows = jnp.where(is_upper(lon), even_up[...], even_low[...])
    south_rows = jnp.where(lat_odd, even_rows, odd_rows)
    north_rows = jnp.where(lat_odd, odd_rows, even_rows)
    far_cols = jnp.where(edge, far_edge[0:48, :], far[...])
    near_cols = near[...]
    west_cols = jnp.where(lon_odd, near_cols, far_cols[0:40])
    east_cols = jnp.where(lon_odd, far_cols[0:40], near_cols)

    q = odd[128:136, :]
    q_west = jnp.where(at_top, swap_pair(q[3:4]), q[2:3])
    q_east = jnp.where(at_top, swap_pair(q[2:3]), q[3:4])
    q_depth = jnp.where(at_top, reversed_lanes(q[0:1]), q[0:1])
    far_even = far_cols[40:41]
    far_odd = jnp.where(edge, jnp.where(lon_odd, q_west, q_east), far_cols[41:42])
    far_odd_d = jnp.where(edge, q_depth, far_cols[43:44])
    near_even, near_even_d = even_rows[132:133], even_rows[133:134]
    near_odd = jnp.where(at_top, swap_pair(beside[0:1]), beside[0:1])
    near_odd_d = jnp.where(at_top, jnp.where(lane1 == 0, shift(beside[1:2], -1), shift(beside[1:2], 1)), beside[1:2])

    def near_depth(row):
        return jnp.where(lon_odd, row[:, 1:2], row[:, 0:1])

    def far_depth(row):
        return jnp.where(lon_odd, row[:, 0:1], row[:, 127:128])

    def by_side(even_part, odd_part):
        return jnp.where(lat_odd, even_part, odd_part), jnp.where(lat_odd, odd_part, even_part)

    def west_east(near_part, far_part):
        return jnp.where(lon_odd, near_part, far_part), jnp.where(lon_odd, far_part, near_part)

    near_s, near_n = by_side(near_even, near_odd)
    far_s, far_n = by_side(far_even, far_odd)
    (sw, se), (nw, ne) = west_east(near_s, far_s), west_east(near_n, far_n)
    near_sd, near_nd = by_side(near_depth(near_even_d), near_depth(near_odd_d))
    far_sd, far_nd = by_side(far_depth(far_cols[42:43]), far_depth(far_odd_d))
    corner_depth = [west_east(near_sd, far_sd), west_east(near_nd, far_nd)]
    odd_west = jnp.where(at_top, swap_pair(odd_info[1:2]), odd_info[0:1])
    odd_east = jnp.where(at_top, swap_pair(odd_info[0:1]), odd_info[1:2])
    own_sw, own_nw = by_side(even_rows[130:131], odd_west)
    own_se, own_ne = by_side(even_rows[131:132], odd_east)

    cols, col_depth = column_groups(packed, depth, west_cols, east_cols)
    cols_s, cols_n, corner_rows = [], [], []
    for out, w, e, own_w, own_e in ((cols_s, sw, se, own_sw, own_se), (cols_n, nw, ne, own_nw, own_ne)):
        for f in range(4):
            x = jnp.where(place1 == 5, shift(w, 4 - 2 * f), shift(e, 2 - 2 * f))
            x = jnp.where(place1 == 6, shift(own_w, 6 - 2 * f), x)
            out.append(jnp.where(place1 == 1, shift(own_e, -2 * f), x))
    for (w, e), own in zip(corner_depth, (south_rows[128:129], north_rows[128:129])):
        x = jnp.where(place1 == 5, w, e)
        x = jnp.where(place1 == 6, own[:, 0:1], x)
        corner_rows.append(jnp.where(place1 == 1, own[:, 127:128], x))

    wets = [
        as_wet(level < x)
        for x in (
            shift(col_depth, -1),
            shift(col_depth, 1),
            north_of(col_depth, corner_rows[1]),
            south_of(col_depth, corner_rows[0]),
        )
    ]
    cols_mid = five_point(
        cols,
        [shift(x, -1) for x in cols],
        [shift(x, 1) for x in cols],
        [north_of(x, y) for x, y in zip(cols, cols_n)],
        [south_of(x, y) for x, y in zip(cols, cols_s)],
        [shift(x, -8) for x in cols[:2]],
        [shift(x, 8) for x in cols[:2]],
        as_wet(level < col_depth),
        wets,
        as_wet(level + 1.0 < col_depth),
        as_wet(jnp.logical_and(lane >= 8, level - 1.0 < col_depth)),
        cosine,
        sine,
    )

    lane16 = lanes_of((LEVELS, LANES))
    sub16 = lax.broadcasted_iota(jnp.int32, (LEVELS, LANES), 0)
    lev16 = sub16.astype(jnp.float32)

    def one_row(c, n, s, ends, ends_d, d0, d_n, d_s, cos_row, sin_row):
        d_w = jnp.where(lane1 == 0, ends_d[0], shift(d0, 1))
        d_e = jnp.where(lane1 == 127, ends_d[1], shift(d0, -1))
        e, w = [], []
        for f in range(4):
            spread_out = jnp.broadcast_to(ends[f], (LEVELS, LANES))
            at_w = jnp.sum(jnp.where(lane16 == 8 * sub16 + 5, spread_out, 0.0), axis=1, keepdims=True)
            at_e = jnp.sum(jnp.where(lane16 == 8 * sub16 + 2, spread_out, 0.0), axis=1, keepdims=True)
            w.append(jnp.where(lane16 == 0, at_w, shift(c[f], 1)))
            e.append(jnp.where(lane16 == 127, at_e, shift(c[f], -1)))
        return five_point(
            c, e, w, n, s,
            [north_of(x, x[15:16]) for x in c[:2]],
            [south_of(x, x[0:1]) for x in c[:2]],
            as_wet(lev16 < d0),
            [as_wet(lev16 < x) for x in (d_e, d_w, d_n, d_s)],
            as_wet(lev16 + 1.0 < d0),
            as_wet(jnp.logical_and(sub16 >= 1, lev16 - 1.0 < d0)),
            cos_row,
            sin_row,
        )

    def of_rows(rows, d):
        at = 64 * d
        return [rows[at + f * 16 : at + f * 16 + 16] for f in range(4)]

    bottom = [x[:, 0, :] for x in fields]
    top = [x[:, ROWS - 1, :] for x in fields]
    south_mid = one_row(
        of_rows(south_rows, 0), bottom, of_rows(south_rows, 1), cols_s, corner_depth[0],
        south_rows[128:129], depth[0:1], south_rows[129:130], angles[64:65, :], angles[66:67, :],
    )
    north_mid = one_row(
        of_rows(north_rows, 0), of_rows(north_rows, 1), top, cols_n, corner_depth[1],
        north_rows[128:129], north_rows[129:130], depth[31:32], angles[65:66, :], angles[67:68, :],
    )

    def outer(top_part, bottom_part):
        return jnp.where(lat_odd, top_part, bottom_part)

    inner = [outer(x[:, ROWS - 2, :], x[:, 1, :]) for x in fields]
    beyond = of_rows(odd_rows, 0)
    inner_d, beyond_d = outer(depth[30:31], depth[1:2]), odd_rows[128:129]
    ends_d = outer(col_depth[31:32], col_depth[0:1])
    outer_mid = one_row(
        [outer(x, y) for x, y in zip(top, bottom)],
        [outer(x, y) for x, y in zip(beyond, inner)],
        [outer(x, y) for x, y in zip(inner, beyond)],
        [outer(x[31:32], x[0:1]) for x in cols],
        (ends_d[:, 5:6], ends_d[:, 2:3]),
        outer(depth[31:32], depth[0:1]),
        outer(beyond_d, inner_d),
        outer(inner_d, beyond_d),
        outer(cosine[31:32], cosine[0:1]),
        outer(sine[31:32], sine[0:1]),
    )

    row = lax.broadcasted_iota(jnp.int32, (ROWS, LANES), 0)
    redone_row = row == outer(ROWS - 1, 0)
    rim = jnp.logical_or(lane == 0, lane == 127)
    rims = [jnp.where(place == 1, x, shift(x, -4)) for x in cols_mid]

    def patched(f, k):
        x = jnp.where(rim, shift(rims[f], 127 - (8 * k + 1)), mid[f, k])
        return jnp.where(redone_row, outer_mid[f][k : k + 1], x)

    outs = (heat_out, salt_out, zonal_out, merid_out)
    copies = []

    def to_out(f, k, value):
        last[f, k] = value
        if k % CHUNK == CHUNK - 1:
            part = pl.ds(k + 1 - CHUNK, CHUNK)
            copy = pltpu.make_async_copy(last.at[f, part], outs[f].at[part], sems.at[f, k // CHUNK])
            copy.start()
            copies.append(copy)

    whole_step(
        patched,
        cols_mid,
        south_mid,
        north_mid,
        to_out,
        depth,
        depths_beside(depth, col_depth, south_rows[128:129], north_rows[128:129]),
        cosine,
        sine,
    )
    for copy in copies:
        copy.wait()


def shapes(*dims):
    return [jax.ShapeDtypeStruct(d, jnp.float32) for d in dims]


def call(kernel, outputs, *operands, scratch=(), held_in=True, held_out=True, grant=32, cost=False):
    vmem, hbm = pl.BlockSpec(memory_space=pltpu.VMEM), pl.BlockSpec(memory_space=pltpu.HBM)
    return pl.pallas_call(
        kernel,
        out_shape=shapes(*outputs),
        in_specs=[vmem if held_in else hbm] * len(operands),
        out_specs=[vmem if held_out else hbm] * len(outputs),
        scratch_shapes=list(scratch),
        cost_estimate=pl.CostEstimate(flops=30_000_000, bytes_accessed=2 << 20, transcendentals=0) if cost else None,
        compiler_params=pltpu.CompilerParams(vmem_limit_bytes=int(grant * 1024 * 1024)),
    )(*operands)


def angle_table():
    first = lax.axis_index("lat") * ROWS
    total = ROWS * N_LAT
    ids = jnp.concatenate([jnp.arange(ROWS), jnp.array([-1, ROWS])]) + first
    ids = jnp.where(ids >= total, 2 * total - 1 - ids, ids)
    angle = ROTATION * (2.0 * (ids.astype(jnp.float32) + 0.5) / total - 1.0)
    c, s = jnp.cos(angle), jnp.sin(angle)
    column = jnp.concatenate([c[:ROWS], s[:ROWS], c[ROWS:], s[ROWS:], jnp.zeros((4,), jnp.float32)])
    return jnp.broadcast_to(column[:, None], (72, LANES))


def on_device(heat, salt, zonal, merid, flag, tally):
    whole = (heat, salt, zonal, merid, flag, tally)
    size = (LEVELS, ROWS, LANES)
    pinned = [pltpu.with_memory_space_constraint(x, pltpu.HBM) for x in whole]
    *fields, depth, packed, info_top, info_bottom, col_near, col_far = call(
        pack_kernel,
        [size] * 4 + [(ROWS, LANES), (4, ROWS, LANES), (8, LANES), (8, LANES), (40, LANES), (40, LANES)],
        *pinned,
        scratch=[pltpu.VMEM((ROWS, LANES), jnp.int32)] * 2 + [pltpu.SemaphoreType.DMA((6,))],
        held_in=False,
    )
    near = send(col_near, near_lon, lambda lat, lon: True)
    rows = call(row_kernel, [(128, LANES)] * 3, *fields)
    row_low, row_odd, row_up = call(join_kernel, [(ROW_MSG, LANES)] * 3, *rows, info_top, info_bottom, near)
    even_low = send(row_low, even_lat, lambda lat, lon: not upper(lon))
    odd = send(row_odd, odd_or_diagonal, lambda lat, lon: lat > 0)
    even_up = send(row_up, even_lat, lambda lat, lon: upper(lon))
    to_far, to_far_edge = call(
        relay_kernel, [(COL_MSG, LANES), (EDGE_MSG, LANES)], even_low, odd, even_up, col_far
    )
    far = send(to_far, far_lon, lambda lat, lon: not is_edge(lat))
    far_edge = send(to_far_edge, far_lon, lambda lat, lon: is_edge(lat))
    known = (*fields, depth, packed, angle_table(), even_low, odd, even_up, near)
    (mid,) = call(early_kernel, [(4,) + size], *known, cost=True)
    return tuple(
        call(
            step_kernel,
            [size] * 4,
            mid, *known, far_edge, far,
            scratch=[
                pltpu.VMEM((ROW_MSG, LANES), jnp.float32),
                pltpu.VMEM((4,) + size, jnp.float32),
                pltpu.SemaphoreType.DMA((4, LEVELS // CHUNK)),
            ],
            held_out=False,
        )
    )


def solution(mesh):
    field, column = P(None, "lat", "lon"), P("lat", "lon")
    return jax.shard_map(
        on_device,
        mesh=mesh,
        in_specs=(field,) * 4 + (column,) * 2,
        out_specs=(field,) * 4,
        check_vma=False,
    )
```

```python
import jax
import jax.numpy as jnp
from jax import lax
from jax.experimental import pallas as pl
from jax.experimental.pallas import tpu as pltpu
from jax.sharding import PartitionSpec as P

MIXING = 0.2
VISCOSITY = 0.05
ROTATION = 0.3
LEVELS = 16
ROWS = 32
LANES = 128
N_LAT = 32
N_LON = 16
BLOCK = 8
ROW_MSG = 136
COL_MSG = 48
CHUNK = 4
FETCHES = 1
EDGE_MSG = COL_MSG + ROW_MSG


def near_lon(lat, lon):
    return lat, lon ^ 1


def far_lon(lat, lon):
    return lat, (lon + 1) % N_LON if lon % 2 else (lon - 1) % N_LON


def even_lat(lat, lon):
    return lat ^ 1, lon


def odd_lat(lat, lon):
    if lat == N_LAT - 1:
        return lat, N_LON - 1 - lon
    return (lat + 1 if lat % 2 else lat - 1), lon


def is_edge(lat):
    return lat > 0 and lat % BLOCK in (0, BLOCK - 1)


def upper(lon):
    return lon // 2 % 2 == 1


def pairs(where_to, member):
    found = []
    for lat in range(N_LAT):
        for lon in range(N_LON):
            if member(lat, lon):
                to_lat, to_lon = where_to(lat, lon)
                found.append((lat * N_LON + lon, to_lat * N_LON + to_lon))
    return found


def send(array, where_to, member):
    return lax.ppermute(array, ("lat", "lon"), pairs(where_to, member))


def odd_or_diagonal(lat, lon):
    to = odd_lat(lat, lon)
    return far_lon(*to) if is_edge(lat) else to


def shift(x, by, axis=1):
    by = by % x.shape[axis]
    return x if by == 0 else pltpu.roll(x, by, axis)


def lanes_of(shape):
    return lax.broadcasted_iota(jnp.int32, shape, 1)


def position():
    return lax.axis_index("lat"), lax.axis_index("lon")


def is_edge_run(lat):
    run = lax.rem(lat, BLOCK)
    return jnp.logical_and(lat > 0, jnp.logical_or(run == 0, run == BLOCK - 1))


def is_upper(lon):
    return lax.rem(lax.div(lon, 2), 2) == 1


def pack_kernel(
    heat_in, salt_in, zonal_in, merid_in, flag_in, tally_in,
    heat, salt, zonal, merid, depth_out, packed, info_top, info_bottom, col_near, col_far,
    flag, tally, sems,
):
    sources, fields = (heat_in, salt_in, zonal_in, merid_in), (heat, salt, zonal, merid)
    copies = [pltpu.make_async_copy(*x, sems.at[i]) for i, x in enumerate(((flag_in, flag), (tally_in, tally)))]
    for i in range(4 * FETCHES):
        part = pl.ds(i % FETCHES * (LEVELS // FETCHES), LEVELS // FETCHES)
        f = i // FETCHES
        copies.append(pltpu.make_async_copy(sources[f].at[part], fields[f].at[part], sems.at[2 + i]))
    for copy in copies:
        copy.start()
    _, lon = position()
    lon_odd = lax.rem(lon, 2) == 1
    copies[0].wait()
    copies[1].wait()
    depth = (flag[...] * tally[...]).astype(jnp.float32)
    depth_out[...] = depth
    lane = lanes_of((ROWS, LANES))
    group = lane >> 3
    pair = (lane & 7) >> 1
    west = jnp.zeros((ROWS, LANES), jnp.float32)
    east = west
    for f, field in enumerate(fields):
        acc = jnp.zeros((ROWS, LANES), jnp.float32)
        for k in range(LEVELS):
            if k % (LEVELS // FETCHES) == 0:
                copies[2 + f * FETCHES + k // (LEVELS // FETCHES)].wait()
            acc = jnp.where(group == k, shift(field[k], 8 * k + 2), acc)
        packed[f] = acc
        west = jnp.where(pair == f, shift(acc, 2 * f - 2), west)
        east = jnp.where(pair == f, shift(acc, 2 * f), east)
    short = lanes_of((8, LANES)) >> 1
    depth_west = jnp.zeros((8, LANES), jnp.float32)
    depth_east = depth_west
    for i in range(4):
        part = depth[8 * i : 8 * i + 8]
        depth_west = jnp.where(short == i, shift(part, 2 * i), depth_west)
        depth_east = jnp.where(short == i, shift(part, 2 * i + 2), depth_east)
    col_near[0:ROWS, :] = jnp.where(lon_odd, west, east)
    col_far[0:ROWS, :] = jnp.where(lon_odd, east, west)
    col_near[ROWS : ROWS + 8, :] = jnp.where(lon_odd, depth_west, depth_east)
    col_far[ROWS : ROWS + 8, :] = jnp.where(lon_odd, depth_east, depth_west)
    blank = jnp.zeros((4, LANES), jnp.float32)
    info_top[...] = jnp.concatenate([depth[31:32], depth[30:31], west[31:32], east[31:32], blank], 0)
    info_bottom[...] = jnp.concatenate([depth[0:1], depth[1:2], west[0:1], east[0:1], blank], 0)


def row_kernel(heat, salt, zonal, merid, low_out, odd_out, up_out):
    lat, _ = position()
    lat_odd = lax.rem(lat, 2) == 1
    for f, field in enumerate((heat, salt, zonal, merid)):
        for d in range(2):
            at = (d * 4 + f) * LEVELS
            top = field[:, ROWS - 1 - d, :]
            bottom = field[:, d, :]
            even = jnp.where(lat_odd, bottom, top)
            low_out[at : at + LEVELS, :] = even
            up_out[at : at + LEVELS, :] = even
            odd_out[at : at + LEVELS, :] = jnp.where(lat_odd, top, bottom)


def join_kernel(low, odd, up, info_top, info_bottom, near, low_out, odd_out, up_out):
    lat, _ = position()
    lat_odd = lax.rem(lat, 2) == 1
    blank = jnp.zeros((2, LANES), jnp.float32)
    top = jnp.concatenate([info_top[0:4, :], near[31:32, :], shift(near[39:40, :], -6), blank], 0)
    bottom = jnp.concatenate([info_bottom[0:4, :], near[0:1, :], near[32:33, :], blank], 0)
    low_out[0:128, :] = low[...]
    up_out[0:128, :] = up[...]
    odd_out[0:128, :] = odd[...]
    even_info = jnp.where(lat_odd, bottom, top)
    low_out[128:136, :] = even_info
    up_out[128:136, :] = even_info
    odd_out[128:136, :] = jnp.where(lat_odd, top, bottom)


def relay_kernel(even_low, odd, even_up, col_far, to_far, to_far_edge):
    _, lon = position()
    lon_odd = lax.rem(lon, 2) == 1
    info_even = jnp.where(is_upper(lon), even_up[128:136, :], even_low[128:136, :])
    info_odd = odd[128:136, :]
    blank = jnp.zeros((4, LANES), jnp.float32)

    def corners(row):
        return jnp.concatenate(
            [info_even[row : row + 1], info_odd[row : row + 1], info_even[0:1], info_odd[0:1], blank], 0
        )

    far_tile = jnp.where(lon_odd, corners(3), corners(2))
    to_far[0:40, :] = col_far[...]
    to_far[40:48, :] = far_tile
    to_far_edge[0:40, :] = col_far[...]
    to_far_edge[40:48, :] = far_tile
    to_far_edge[48:184, :] = odd[...]


def near_kernel(even_low, odd, even_up, far_edge, col_near, _, to_near):
    lat, lon = position()
    lon_odd = lax.rem(lon, 2) == 1
    at_top = lat == N_LAT - 1
    even_info = jnp.where(is_upper(lon), even_up[128:136, :], even_low[128:136, :])
    odd_info = jnp.where(is_edge_run(lat), far_edge[176:184, :], odd[128:136, :])

    def beside(info, first):
        return jnp.where(first, info[2:3], info[3:4]), jnp.where(first, info[0:1], shift(info[0:1], 2))

    to_near[0:40, :] = col_near[...]
    blank = jnp.zeros((4, LANES), jnp.float32)
    to_near[40:48, :] = jnp.concatenate(
        [*beside(even_info, lon_odd), *beside(odd_info, jnp.logical_xor(lon_odd, at_top)), blank], 0
    )


def reversed_lanes(x):
    lane = lanes_of(x.shape)
    for b in range(7):
        x = jnp.where((lane >> b) & 1 == 1, shift(x, 1 << b), shift(x, -(1 << b)))
    return x


def five_point(c, e, w, n, s, up, down, wet, wets, wet_up, wet_down, cosine, sine):
    wet_e, wet_w, wet_n, wet_s = (wet * x for x in wets)
    flow_e = 0.5 * (c[2] + e[2]) * wet_e
    flow_w = 0.5 * (c[2] + w[2]) * wet_w
    flow_n = 0.5 * (c[3] + n[3]) * wet_n
    flow_s = 0.5 * (c[3] + s[3]) * wet_s

    def gain(f, viscosity):
        east = (jnp.maximum(flow_e, 0.0) * c[f] + jnp.minimum(flow_e, 0.0) * e[f]) - viscosity * wet_e * (e[f] - c[f])
        west = (jnp.maximum(flow_w, 0.0) * w[f] + jnp.minimum(flow_w, 0.0) * c[f]) - viscosity * wet_w * (c[f] - w[f])
        north = (jnp.maximum(flow_n, 0.0) * c[f] + jnp.minimum(flow_n, 0.0) * n[f]) - viscosity * wet_n * (n[f] - c[f])
        south = (jnp.maximum(flow_s, 0.0) * s[f] + jnp.minimum(flow_s, 0.0) * c[f]) - viscosity * wet_s * (c[f] - s[f])
        return c[f] - ((east - west) + (north - south))

    def tracer(f):
        mixed = MIXING * ((up[f] - c[f]) * (wet * wet_up) - (c[f] - down[f]) * (wet * wet_down))
        return wet * (gain(f, 0.0) + mixed)

    ua, va = gain(2, VISCOSITY), gain(3, VISCOSITY)
    return [tracer(0), tracer(1), wet * (cosine * ua + sine * va), wet * (cosine * va - sine * ua)]


def north_of(x, last):
    return jnp.concatenate([x[1:], last], 0)


def south_of(x, first):
    return jnp.concatenate([first, x[:-1]], 0)


def as_wet(mask):
    return jnp.where(mask, 1.0, 0.0)


def column_groups(packed, depth, west_cols, east_cols):
    lane = lanes_of((ROWS, LANES))
    place = lane & 7
    cols = []
    for f in range(4):
        own = packed[f]
        x = jnp.where(place < 2, own, shift(own, 4))
        x = jnp.where((place >> 1) == 1, shift(east_cols[0:32], 2 - 2 * f), x)
        cols.append(jnp.where((place >> 1) == 2, shift(west_cols[0:32], 4 - 2 * f), x))
    west_d = jnp.concatenate([shift(west_cols[32:40], 4 - 2 * i) for i in range(4)], 0)
    east_d = jnp.concatenate([shift(east_cols[32:40], 2 - 2 * i) for i in range(4)], 0)
    col_depth = jnp.where(lane < 2, shift(depth, 2), shift(depth, 6))
    col_depth = jnp.where((lane >> 1) == 1, east_d, col_depth)
    col_depth = jnp.where((lane >> 1) == 2, west_d, col_depth)
    col_depth = jnp.where(lane < 8, col_depth, 0.0)
    for b in (8, 16, 32, 64):
        col_depth = col_depth + shift(col_depth, b)
    return cols, col_depth


def depths_beside(depth, col_depth, south, north):
    lane = lanes_of((ROWS, LANES))
    return (
        jnp.where(lane == 127, shift(col_depth, 125), shift(depth, -1)),
        jnp.where(lane == 0, shift(col_depth, 123), shift(depth, 1)),
        north_of(depth, north),
        south_of(depth, south),
    )


def whole_step(read, col_values, rows_s, rows_n, write, depth, beside, cosine, sine):
    lane = lanes_of((ROWS, LANES))
    place = lane & 7
    row = lax.broadcasted_iota(jnp.int32, (ROWS, LANES), 0)
    first_row, last_row = row == 0, row == ROWS - 1
    m_e, m_w, m_n, m_s = (jnp.minimum(depth, x) for x in beside)
    sides = [jnp.where(place == 2, x, shift(x, -2)) for x in col_values]
    now = [read(f, 0) for f in range(4)]
    carried = [None, None]
    for k in range(LEVELS):
        above = [read(f, k + 1) for f in range(4)] if k + 1 < LEVELS else None
        half_e, half_w, half_n, half_s = (jnp.where(k < x, 0.5, 0.0) for x in (m_e, m_w, m_n, m_s))
        e, w, n, s = [], [], [], []
        for f in range(4):
            x = now[f]
            ends = shift(sides[f], 127 - (8 * k + 2))
            e.append(jnp.where(lane == 127, ends, shift(x, -1)))
            w.append(jnp.where(lane == 0, ends, shift(x, 1)))
            n.append(jnp.where(last_row, rows_n[f][k : k + 1], shift(x, -1, 0)))
            s.append(jnp.where(first_row, rows_s[f][k : k + 1], shift(x, 1, 0)))
        flow_e = (now[2] + e[2]) * half_e
        flow_w = (now[2] + w[2]) * half_w
        flow_n = (now[3] + n[3]) * half_n
        flow_s = (now[3] + s[3]) * half_s
        out_e, in_e = jnp.maximum(flow_e, 0.0), jnp.minimum(flow_e, 0.0)
        in_w, out_w = jnp.maximum(flow_w, 0.0), jnp.minimum(flow_w, 0.0)
        out_n, in_n = jnp.maximum(flow_n, 0.0), jnp.minimum(flow_n, 0.0)
        in_s, out_s = jnp.maximum(flow_s, 0.0), jnp.minimum(flow_s, 0.0)
        kept = 1.0 - ((out_e - out_w) + (out_n - out_s))
        wet = k < depth
        new = []
        for f in range(2):
            x = now[f]
            total = (x * kept - (in_e * e[f] - in_w * w[f])) - (in_n * n[f] - in_s * s[f])
            if above is not None:
                flux = jnp.where(k + 1 < depth, MIXING * (above[f] - x), 0.0)
                total = total + flux
            if carried[f] is not None:
                total = total - carried[f]
            if above is not None:
                carried[f] = flux
            new.append(jnp.where(wet, total, 0.0))
        thick = 2.0 * VISCOSITY
        vis_e, vis_w, vis_n, vis_s = (thick * x for x in (half_e, half_w, half_n, half_s))
        kept = kept - ((vis_e + vis_w) + (vis_n + vis_s))
        in_e, in_w, in_n, in_s = vis_e - in_e, vis_w + in_w, vis_n - in_n, vis_s + in_s
        ua, va = (
            (now[f] * kept + (in_e * e[f] + in_w * w[f])) + (in_n * n[f] + in_s * s[f]) for f in (2, 3)
        )
        new.append(jnp.where(wet, cosine * ua + sine * va, 0.0))
        new.append(jnp.where(wet, cosine * va - sine * ua, 0.0))
        for f in range(4):
            write(f, k, new[f])
        now = above


def early_kernel(
    heat, salt, zonal, merid, depth_in, packed, angles, even_low, odd, even_up, near, mid_out
):
    lat, lon = position()
    lat_odd = lax.rem(lat, 2) == 1
    lon_odd = lax.rem(lon, 2) == 1
    fields = (heat, salt, zonal, merid)
    depth = depth_in[...]
    even_rows = jnp.where(is_upper(lon), even_up[...], even_low[...])
    odd_rows = odd[...]
    south_rows = jnp.where(lat_odd, even_rows, odd_rows)
    north_rows = jnp.where(lat_odd, odd_rows, even_rows)
    near_cols = near[...]
    west_cols = jnp.where(lon_odd, near_cols, 0.0)
    east_cols = jnp.where(lon_odd, 0.0, near_cols)
    cols, col_depth = column_groups(packed, depth, west_cols, east_cols)

    def write(f, k, value):
        mid_out[f, k] = value

    whole_step(
        lambda f, k: fields[f][k],
        cols,
        [south_rows[f * 16 : f * 16 + 16] for f in range(4)],
        [north_rows[f * 16 : f * 16 + 16] for f in range(4)],
        write,
        depth,
        depths_beside(depth, col_depth, south_rows[128:129], north_rows[128:129]),
        angles[0:32, :],
        angles[32:64, :],
    )


def step_kernel(
    mid, heat, salt, zonal, merid, depth_in, packed, angles, even_low, odd, even_up, near, near_up, far_edge, far,
    heat_out, salt_out, zonal_out, merid_out, turned, last, sems,
):
    lat, lon = position()
    lat_odd = lax.rem(lat, 2) == 1
    lon_odd = lax.rem(lon, 2) == 1
    at_top = lat == N_LAT - 1
    edge = is_edge_run(lat)
    late = is_upper(lon)
    fields = (heat, salt, zonal, merid)
    lane = lanes_of((ROWS, LANES))
    place = lane & 7
    level = (lane >> 3).astype(jnp.float32)
    lane1 = lanes_of((1, LANES))
    place1 = lane1 & 7
    depth = depth_in[...]
    cosine, sine = angles[0:32, :], angles[32:64, :]

    signs = jnp.where(jnp.logical_and(at_top, place1 >= 4), -1.0, 1.0)

    def swap_pair(x):
        return jnp.where(lane1 & 1 == 1, shift(x, 1), shift(x, -1)) * signs

    odd_rows = jnp.where(edge, far_edge[48:184, :], odd[...])
    beside = odd_rows[132:134]
    turned[...] = odd_rows

    @pl.when(at_top)
    def _():
        for at in range(0, 130, 16):
            part = reversed_lanes(odd_rows[at : min(at + 16, 130)])
            turned[at : min(at + 16, 130), :] = -part if at < 128 and at // 16 % 4 >= 2 else part

    even_rows = jnp.where(is_upper(lon), even_up[...], even_low[...])
    even_beside = jnp.where(late, near_up[40:42, :], even_rows[132:134])
    beside = jnp.where(late, near_up[42:44, :], beside)
    odd_info = odd_rows[130:132]
    odd_rows = turned[...]
    south_rows = jnp.where(lat_odd, even_rows, odd_rows)
    north_rows = jnp.where(lat_odd, odd_rows, even_rows)
    far_cols = jnp.where(edge, far_edge[0:48, :], far[...])
    near_cols = jnp.where(late, near_up[0:40, :], near[...])
    west_cols = jnp.where(lon_odd, near_cols, far_cols[0:40])
    east_cols = jnp.where(lon_odd, far_cols[0:40], near_cols)

    q = odd[128:136, :]
    q_west = jnp.where(at_top, swap_pair(q[3:4]), q[2:3])
    q_east = jnp.where(at_top, swap_pair(q[2:3]), q[3:4])
    q_depth = jnp.where(at_top, reversed_lanes(q[0:1]), q[0:1])
    far_even = far_cols[40:41]
    far_odd = jnp.where(edge, jnp.where(lon_odd, q_west, q_east), far_cols[41:42])
    far_odd_d = jnp.where(edge, q_depth, far_cols[43:44])
    near_even, near_even_d = even_beside[0:1], even_beside[1:2]
    near_odd = jnp.where(at_top, swap_pair(beside[0:1]), beside[0:1])
    near_odd_d = jnp.where(at_top, jnp.where(lane1 == 0, shift(beside[1:2], -1), shift(beside[1:2], 1)), beside[1:2])

    def near_depth(row):
        return jnp.where(lon_odd, row[:, 1:2], row[:, 0:1])

    def far_depth(row):
        return jnp.where(lon_odd, row[:, 0:1], row[:, 127:128])

    def by_side(even_part, odd_part):
        return jnp.where(lat_odd, even_part, odd_part), jnp.where(lat_odd, odd_part, even_part)

    def west_east(near_part, far_part):
        return jnp.where(lon_odd, near_part, far_part), jnp.where(lon_odd, far_part, near_part)

    near_s, near_n = by_side(near_even, near_odd)
    far_s, far_n = by_side(far_even, far_odd)
    (sw, se), (nw, ne) = west_east(near_s, far_s), west_east(near_n, far_n)
    near_sd, near_nd = by_side(near_depth(near_even_d), near_depth(near_odd_d))
    far_sd, far_nd = by_side(far_depth(far_cols[42:43]), far_depth(far_odd_d))
    corner_depth = [west_east(near_sd, far_sd), west_east(near_nd, far_nd)]
    odd_west = jnp.where(at_top, swap_pair(odd_info[1:2]), odd_info[0:1])
    odd_east = jnp.where(at_top, swap_pair(odd_info[0:1]), odd_info[1:2])
    own_sw, own_nw = by_side(even_rows[130:131], odd_west)
    own_se, own_ne = by_side(even_rows[131:132], odd_east)

    cols, col_depth = column_groups(packed, depth, west_cols, east_cols)
    cols_s, cols_n, corner_rows = [], [], []
    for out, w, e, own_w, own_e in ((cols_s, sw, se, own_sw, own_se), (cols_n, nw, ne, own_nw, own_ne)):
        for f in range(4):
            x = jnp.where(place1 == 5, shift(w, 4 - 2 * f), shift(e, 2 - 2 * f))
            x = jnp.where(place1 == 6, shift(own_w, 6 - 2 * f), x)
            out.append(jnp.where(place1 == 1, shift(own_e, -2 * f), x))
    for (w, e), own in zip(corner_depth, (south_rows[128:129], north_rows[128:129])):
        x = jnp.where(place1 == 5, w, e)
        x = jnp.where(place1 == 6, own[:, 0:1], x)
        corner_rows.append(jnp.where(place1 == 1, own[:, 127:128], x))

    wets = [
        as_wet(level < x)
        for x in (
            shift(col_depth, -1),
            shift(col_depth, 1),
            north_of(col_depth, corner_rows[1]),
            south_of(col_depth, corner_rows[0]),
        )
    ]
    cols_mid = five_point(
        cols,
        [shift(x, -1) for x in cols],
        [shift(x, 1) for x in cols],
        [north_of(x, y) for x, y in zip(cols, cols_n)],
        [south_of(x, y) for x, y in zip(cols, cols_s)],
        [shift(x, -8) for x in cols[:2]],
        [shift(x, 8) for x in cols[:2]],
        as_wet(level < col_depth),
        wets,
        as_wet(level + 1.0 < col_depth),
        as_wet(jnp.logical_and(lane >= 8, level - 1.0 < col_depth)),
        cosine,
        sine,
    )

    lane16 = lanes_of((LEVELS, LANES))
    sub16 = lax.broadcasted_iota(jnp.int32, (LEVELS, LANES), 0)
    lev16 = sub16.astype(jnp.float32)

    def one_row(c, n, s, ends, ends_d, d0, d_n, d_s, cos_row, sin_row):
        d_w = jnp.where(lane1 == 0, ends_d[0], shift(d0, 1))
        d_e = jnp.where(lane1 == 127, ends_d[1], shift(d0, -1))
        e, w = [], []
        for f in range(4):
            spread_out = jnp.broadcast_to(ends[f], (LEVELS, LANES))
            at_w = jnp.sum(jnp.where(lane16 == 8 * sub16 + 5, spread_out, 0.0), axis=1, keepdims=True)
            at_e = jnp.sum(jnp.where(lane16 == 8 * sub16 + 2, spread_out, 0.0), axis=1, keepdims=True)
            w.append(jnp.where(lane16 == 0, at_w, shift(c[f], 1)))
            e.append(jnp.where(lane16 == 127, at_e, shift(c[f], -1)))
        return five_point(
            c, e, w, n, s,
            [north_of(x, x[15:16]) for x in c[:2]],
            [south_of(x, x[0:1]) for x in c[:2]],
            as_wet(lev16 < d0),
            [as_wet(lev16 < x) for x in (d_e, d_w, d_n, d_s)],
            as_wet(lev16 + 1.0 < d0),
            as_wet(jnp.logical_and(sub16 >= 1, lev16 - 1.0 < d0)),
            cos_row,
            sin_row,
        )

    def of_rows(rows, d):
        at = 64 * d
        return [rows[at + f * 16 : at + f * 16 + 16] for f in range(4)]

    bottom = [x[:, 0, :] for x in fields]
    top = [x[:, ROWS - 1, :] for x in fields]
    south_mid = one_row(
        of_rows(south_rows, 0), bottom, of_rows(south_rows, 1), cols_s, corner_depth[0],
        south_rows[128:129], depth[0:1], south_rows[129:130], angles[64:65, :], angles[66:67, :],
    )
    north_mid = one_row(
        of_rows(north_rows, 0), of_rows(north_rows, 1), top, cols_n, corner_depth[1],
        north_rows[128:129], north_rows[129:130], depth[31:32], angles[65:66, :], angles[67:68, :],
    )

    def outer(top_part, bottom_part):
        return jnp.where(lat_odd, top_part, bottom_part)

    inner = [outer(x[:, ROWS - 2, :], x[:, 1, :]) for x in fields]
    beyond = of_rows(odd_rows, 0)
    inner_d, beyond_d = outer(depth[30:31], depth[1:2]), odd_rows[128:129]
    ends_d = outer(col_depth[31:32], col_depth[0:1])
    outer_mid = one_row(
        [outer(x, y) for x, y in zip(top, bottom)],
        [outer(x, y) for x, y in zip(beyond, inner)],
        [outer(x, y) for x, y in zip(inner, beyond)],
        [outer(x[31:32], x[0:1]) for x in cols],
        (ends_d[:, 5:6], ends_d[:, 2:3]),
        outer(depth[31:32], depth[0:1]),
        outer(beyond_d, inner_d),
        outer(inner_d, beyond_d),
        outer(cosine[31:32], cosine[0:1]),
        outer(sine[31:32], sine[0:1]),
    )

    row = lax.broadcasted_iota(jnp.int32, (ROWS, LANES), 0)
    redone_row = row == outer(ROWS - 1, 0)
    rim = jnp.logical_or(lane == 0, lane == 127)
    rims = [jnp.where(place == 1, x, shift(x, -4)) for x in cols_mid]

    def patched(f, k):
        x = jnp.where(rim, shift(rims[f], 127 - (8 * k + 1)), mid[f, k])
        return jnp.where(redone_row, outer_mid[f][k : k + 1], x)

    outs = (heat_out, salt_out, zonal_out, merid_out)
    copies = []

    def to_out(f, k, value):
        last[f, k] = value
        if k % CHUNK == CHUNK - 1:
            part = pl.ds(k + 1 - CHUNK, CHUNK)
            copy = pltpu.make_async_copy(last.at[f, part], outs[f].at[part], sems.at[f, k // CHUNK])
            copy.start()
            copies.append(copy)

    whole_step(
        patched,
        cols_mid,
        south_mid,
        north_mid,
        to_out,
        depth,
        depths_beside(depth, col_depth, south_rows[128:129], north_rows[128:129]),
        cosine,
        sine,
    )
    for copy in copies:
        copy.wait()


def shapes(*dims):
    return [jax.ShapeDtypeStruct(d, jnp.float32) for d in dims]


def call(kernel, outputs, *operands, scratch=(), held_in=True, held_out=True, grant=32, cost=False):
    vmem, hbm = pl.BlockSpec(memory_space=pltpu.VMEM), pl.BlockSpec(memory_space=pltpu.HBM)
    return pl.pallas_call(
        kernel,
        out_shape=shapes(*outputs),
        in_specs=[vmem if held_in else hbm] * len(operands),
        out_specs=[vmem if held_out else hbm] * len(outputs),
        scratch_shapes=list(scratch),
        cost_estimate=pl.CostEstimate(flops=30_000_000, bytes_accessed=2 << 20, transcendentals=0) if cost else None,
        compiler_params=pltpu.CompilerParams(vmem_limit_bytes=int(grant * 1024 * 1024)),
    )(*operands)


def angle_table():
    first = lax.axis_index("lat") * ROWS
    total = ROWS * N_LAT
    ids = jnp.concatenate([jnp.arange(ROWS), jnp.array([-1, ROWS])]) + first
    ids = jnp.where(ids >= total, 2 * total - 1 - ids, ids)
    angle = ROTATION * (2.0 * (ids.astype(jnp.float32) + 0.5) / total - 1.0)
    c, s = jnp.cos(angle), jnp.sin(angle)
    column = jnp.concatenate([c[:ROWS], s[:ROWS], c[ROWS:], s[ROWS:], jnp.zeros((4,), jnp.float32)])
    return jnp.broadcast_to(column[:, None], (72, LANES))


def on_device(heat, salt, zonal, merid, flag, tally):
    whole = (heat, salt, zonal, merid, flag, tally)
    size = (LEVELS, ROWS, LANES)
    pinned = [pltpu.with_memory_space_constraint(x, pltpu.HBM) for x in whole]
    *fields, depth, packed, info_top, info_bottom, col_near, col_far = call(
        pack_kernel,
        [size] * 4 + [(ROWS, LANES), (4, ROWS, LANES), (8, LANES), (8, LANES), (40, LANES), (40, LANES)],
        *pinned,
        scratch=[pltpu.VMEM((ROWS, LANES), jnp.int32)] * 2 + [pltpu.SemaphoreType.DMA((2 + 4 * FETCHES,))],
        held_in=False,
    )
    near = send(col_near, near_lon, lambda lat, lon: not upper(lon) or lat == N_LAT - 1)
    rows = call(row_kernel, [(128, LANES)] * 3, *fields)
    row_low, row_odd, row_up = call(join_kernel, [(ROW_MSG, LANES)] * 3, *rows, info_top, info_bottom, near)
    even_low = send(row_low, even_lat, lambda lat, lon: not upper(lon))
    odd = send(row_odd, odd_or_diagonal, lambda lat, lon: lat > 0)
    even_up = send(row_up, even_lat, lambda lat, lon: upper(lon))
    to_far, to_far_edge = call(
        relay_kernel, [(COL_MSG, LANES), (EDGE_MSG, LANES)], even_low, odd, even_up, col_far
    )
    far = send(to_far, far_lon, lambda lat, lon: not is_edge(lat))
    far_edge = send(to_far_edge, far_lon, lambda lat, lon: is_edge(lat))
    known = (*fields, depth, packed, angle_table(), even_low, odd, even_up, near)
    (mid,) = call(early_kernel, [(4,) + size], *known, cost=True)
    (to_near,) = call(near_kernel, [(COL_MSG, LANES)], even_low, odd, even_up, far_edge, col_near, mid)
    near_up = send(to_near, near_lon, lambda lat, lon: upper(lon))
    return tuple(
        call(
            step_kernel,
            [size] * 4,
            mid, *known, near_up, far_edge, far,
            scratch=[
                pltpu.VMEM((ROW_MSG, LANES), jnp.float32),
                pltpu.VMEM((4,) + size, jnp.float32),
                pltpu.SemaphoreType.DMA((4, LEVELS // CHUNK)),
            ],
            held_out=False,
        )
    )


def solution(mesh):
    field, column = P(None, "lat", "lon"), P("lat", "lon")
    return jax.shard_map(
        on_device,
        mesh=mesh,
        in_specs=(field,) * 4 + (column,) * 2,
        out_specs=(field,) * 4,
        check_vma=False,
    )
```

```python
import jax
import jax.numpy as jnp
from jax import lax
from jax.experimental import pallas as pl
from jax.experimental.pallas import tpu as pltpu
from jax.sharding import PartitionSpec as P

MIXING = 0.2
VISCOSITY = 0.05
ROTATION = 0.3
LEVELS = 16
ROWS = 32
LANES = 128
N_LAT = 32
N_LON = 16
BLOCK = 8
ROW_MSG = 136
COL_MSG = 48
CHUNK = 8
EDGE_MSG = COL_MSG + ROW_MSG


def near_lon(lat, lon):
    return lat, lon ^ 1


def far_lon(lat, lon):
    return lat, (lon + 1) % N_LON if lon % 2 else (lon - 1) % N_LON


def even_lat(lat, lon):
    return lat ^ 1, lon


def odd_lat(lat, lon):
    if lat == N_LAT - 1:
        return lat, N_LON - 1 - lon
    return (lat + 1 if lat % 2 else lat - 1), lon


def is_edge(lat):
    return lat > 0 and lat % BLOCK in (0, BLOCK - 1)


def upper(lon):
    return lon // 2 % 2 == 1


def meets_even_early(lat, lon):
    return not upper(lon) and lat % BLOCK < BLOCK // 2


def pairs(where_to, member):
    found = []
    for lat in range(N_LAT):
        for lon in range(N_LON):
            if member(lat, lon):
                to_lat, to_lon = where_to(lat, lon)
                found.append((lat * N_LON + lon, to_lat * N_LON + to_lon))
    return found


def send(array, where_to, member):
    return lax.ppermute(array, ("lat", "lon"), pairs(where_to, member))


def odd_or_diagonal(lat, lon):
    to = odd_lat(lat, lon)
    return far_lon(*to) if is_edge(lat) else to


def shift(x, by, axis=1):
    by = by % x.shape[axis]
    return x if by == 0 else pltpu.roll(x, by, axis)


def lanes_of(shape):
    return lax.broadcasted_iota(jnp.int32, shape, 1)


def position():
    return lax.axis_index("lat"), lax.axis_index("lon")


def is_edge_run(lat):
    run = lax.rem(lat, BLOCK)
    return jnp.logical_and(lat > 0, jnp.logical_or(run == 0, run == BLOCK - 1))


def is_upper(lon):
    return lax.rem(lax.div(lon, 2), 2) == 1


def is_late_even(lat, lon):
    return jnp.logical_or(is_upper(lon), lax.rem(lat, BLOCK) >= BLOCK // 2)


def pack_kernel(
    heat_in, salt_in, zonal_in, merid_in, flag_in, tally_in,
    heat, salt, zonal, merid, depth_out, packed, info_top, info_bottom, col_near, col_far,
    flag, tally, sems,
):
    sources, fields = (heat_in, salt_in, zonal_in, merid_in), (heat, salt, zonal, merid)
    pairs_in = [*zip(sources, fields), (flag_in, flag), (tally_in, tally)]
    copies = [pltpu.make_async_copy(*x, sems.at[i]) for i, x in enumerate(pairs_in)]
    for copy in copies:
        copy.start()
    _, lon = position()
    lon_odd = lax.rem(lon, 2) == 1
    lane = lanes_of((ROWS, LANES))
    group = lane >> 3
    pair = (lane & 7) >> 1
    west = jnp.zeros((ROWS, LANES), jnp.float32)
    east = west
    for f, field in enumerate(fields):
        copies[f].wait()
        acc = jnp.zeros((ROWS, LANES), jnp.float32)
        for k in range(LEVELS):
            acc = jnp.where(group == k, shift(field[k], 8 * k + 2), acc)
        packed[f] = acc
        west = jnp.where(pair == f, shift(acc, 2 * f - 2), west)
        east = jnp.where(pair == f, shift(acc, 2 * f), east)
    copies[4].wait()
    copies[5].wait()
    depth = (flag[...] * tally[...]).astype(jnp.float32)
    depth_out[...] = depth
    short = lanes_of((8, LANES)) >> 1
    depth_west = jnp.zeros((8, LANES), jnp.float32)
    depth_east = depth_west
    for i in range(4):
        part = depth[8 * i : 8 * i + 8]
        depth_west = jnp.where(short == i, shift(part, 2 * i), depth_west)
        depth_east = jnp.where(short == i, shift(part, 2 * i + 2), depth_east)
    col_near[0:ROWS, :] = jnp.where(lon_odd, west, east)
    col_far[0:ROWS, :] = jnp.where(lon_odd, east, west)
    col_near[ROWS : ROWS + 8, :] = jnp.where(lon_odd, depth_west, depth_east)
    col_far[ROWS : ROWS + 8, :] = jnp.where(lon_odd, depth_east, depth_west)
    blank = jnp.zeros((4, LANES), jnp.float32)
    info_top[...] = jnp.concatenate([depth[31:32], depth[30:31], west[31:32], east[31:32], blank], 0)
    info_bottom[...] = jnp.concatenate([depth[0:1], depth[1:2], west[0:1], east[0:1], blank], 0)


def row_kernel(heat, salt, zonal, merid, low_out, odd_out, up_out):
    lat, _ = position()
    lat_odd = lax.rem(lat, 2) == 1
    for f, field in enumerate((heat, salt, zonal, merid)):
        for d in range(2):
            at = (d * 4 + f) * LEVELS
            top = field[:, ROWS - 1 - d, :]
            bottom = field[:, d, :]
            even = jnp.where(lat_odd, bottom, top)
            low_out[at : at + LEVELS, :] = even
            up_out[at : at + LEVELS, :] = even
            odd_out[at : at + LEVELS, :] = jnp.where(lat_odd, top, bottom)


def join_kernel(low, odd, up, info_top, info_bottom, near, low_out, odd_out, up_out):
    lat, _ = position()
    lat_odd = lax.rem(lat, 2) == 1
    blank = jnp.zeros((2, LANES), jnp.float32)
    top = jnp.concatenate([info_top[0:4, :], near[31:32, :], shift(near[39:40, :], -6), blank], 0)
    bottom = jnp.concatenate([info_bottom[0:4, :], near[0:1, :], near[32:33, :], blank], 0)
    low_out[0:128, :] = low[...]
    up_out[0:128, :] = up[...]
    odd_out[0:128, :] = odd[...]
    even_info = jnp.where(lat_odd, bottom, top)
    low_out[128:136, :] = even_info
    up_out[128:136, :] = even_info
    odd_out[128:136, :] = jnp.where(lat_odd, top, bottom)


def relay_kernel(even_low, odd, even_up, col_far, to_far, to_far_edge):
    lat, lon = position()
    lon_odd = lax.rem(lon, 2) == 1
    info_even = jnp.where(is_late_even(lat, lon), even_up[128:136, :], even_low[128:136, :])
    info_odd = odd[128:136, :]
    blank = jnp.zeros((4, LANES), jnp.float32)

    def corners(row):
        return jnp.concatenate(
            [info_even[row : row + 1], info_odd[row : row + 1], info_even[0:1], info_odd[0:1], blank], 0
        )

    far_tile = jnp.where(lon_odd, corners(3), corners(2))
    to_far[0:40, :] = col_far[...]
    to_far[40:48, :] = far_tile
    to_far_edge[0:40, :] = col_far[...]
    to_far_edge[40:48, :] = far_tile
    to_far_edge[48:184, :] = odd[...]


def near_kernel(even_low, odd, even_up, far_edge, col_near, _, to_near):
    lat, lon = position()
    lon_odd = lax.rem(lon, 2) == 1
    at_top = lat == N_LAT - 1
    even_info = jnp.where(is_late_even(lat, lon), even_up[128:136, :], even_low[128:136, :])
    odd_info = jnp.where(is_edge_run(lat), far_edge[176:184, :], odd[128:136, :])

    def beside(info, first):
        return jnp.where(first, info[2:3], info[3:4]), jnp.where(first, info[0:1], shift(info[0:1], 2))

    to_near[0:40, :] = col_near[...]
    blank = jnp.zeros((4, LANES), jnp.float32)
    to_near[40:48, :] = jnp.concatenate(
        [*beside(even_info, lon_odd), *beside(odd_info, jnp.logical_xor(lon_odd, at_top)), blank], 0
    )


def reversed_lanes(x):
    lane = lanes_of(x.shape)
    for b in range(7):
        x = jnp.where((lane >> b) & 1 == 1, shift(x, 1 << b), shift(x, -(1 << b)))
    return x


def five_point(c, e, w, n, s, up, down, wet, wets, wet_up, wet_down, cosine, sine):
    wet_e, wet_w, wet_n, wet_s = (wet * x for x in wets)
    flow_e = 0.5 * (c[2] + e[2]) * wet_e
    flow_w = 0.5 * (c[2] + w[2]) * wet_w
    flow_n = 0.5 * (c[3] + n[3]) * wet_n
    flow_s = 0.5 * (c[3] + s[3]) * wet_s

    def gain(f, viscosity):
        east = (jnp.maximum(flow_e, 0.0) * c[f] + jnp.minimum(flow_e, 0.0) * e[f]) - viscosity * wet_e * (e[f] - c[f])
        west = (jnp.maximum(flow_w, 0.0) * w[f] + jnp.minimum(flow_w, 0.0) * c[f]) - viscosity * wet_w * (c[f] - w[f])
        north = (jnp.maximum(flow_n, 0.0) * c[f] + jnp.minimum(flow_n, 0.0) * n[f]) - viscosity * wet_n * (n[f] - c[f])
        south = (jnp.maximum(flow_s, 0.0) * s[f] + jnp.minimum(flow_s, 0.0) * c[f]) - viscosity * wet_s * (c[f] - s[f])
        return c[f] - ((east - west) + (north - south))

    def tracer(f):
        mixed = MIXING * ((up[f] - c[f]) * (wet * wet_up) - (c[f] - down[f]) * (wet * wet_down))
        return wet * (gain(f, 0.0) + mixed)

    ua, va = gain(2, VISCOSITY), gain(3, VISCOSITY)
    return [tracer(0), tracer(1), wet * (cosine * ua + sine * va), wet * (cosine * va - sine * ua)]


def north_of(x, last):
    return jnp.concatenate([x[1:], last], 0)


def south_of(x, first):
    return jnp.concatenate([first, x[:-1]], 0)


def as_wet(mask):
    return jnp.where(mask, 1.0, 0.0)


def column_groups(packed, depth, west_cols, east_cols):
    lane = lanes_of((ROWS, LANES))
    place = lane & 7
    cols = []
    for f in range(4):
        own = packed[f]
        x = jnp.where(place < 2, own, shift(own, 4))
        x = jnp.where((place >> 1) == 1, shift(east_cols[0:32], 2 - 2 * f), x)
        cols.append(jnp.where((place >> 1) == 2, shift(west_cols[0:32], 4 - 2 * f), x))
    west_d = jnp.concatenate([shift(west_cols[32:40], 4 - 2 * i) for i in range(4)], 0)
    east_d = jnp.concatenate([shift(east_cols[32:40], 2 - 2 * i) for i in range(4)], 0)
    col_depth = jnp.where(lane < 2, shift(depth, 2), shift(depth, 6))
    col_depth = jnp.where((lane >> 1) == 1, east_d, col_depth)
    col_depth = jnp.where((lane >> 1) == 2, west_d, col_depth)
    col_depth = jnp.where(lane < 8, col_depth, 0.0)
    for b in (8, 16, 32, 64):
        col_depth = col_depth + shift(col_depth, b)
    return cols, col_depth


def depths_beside(depth, col_depth, south, north):
    lane = lanes_of((ROWS, LANES))
    return (
        jnp.where(lane == 127, shift(col_depth, 125), shift(depth, -1)),
        jnp.where(lane == 0, shift(col_depth, 123), shift(depth, 1)),
        north_of(depth, north),
        south_of(depth, south),
    )


def whole_step(read, col_values, rows_s, rows_n, write, depth, beside, cosine, sine):
    lane = lanes_of((ROWS, LANES))
    place = lane & 7
    row = lax.broadcasted_iota(jnp.int32, (ROWS, LANES), 0)
    first_row, last_row = row == 0, row == ROWS - 1
    m_e, m_w, m_n, m_s = (jnp.minimum(depth, x) for x in beside)
    sides = [jnp.where(place == 2, x, shift(x, -2)) for x in col_values]
    now = [read(f, 0) for f in range(4)]
    carried = [None, None]
    for k in range(LEVELS):
        above = [read(f, k + 1) for f in range(4)] if k + 1 < LEVELS else None
        half_e, half_w, half_n, half_s = (jnp.where(k < x, 0.5, 0.0) for x in (m_e, m_w, m_n, m_s))
        e, w, n, s = [], [], [], []
        for f in range(4):
            x = now[f]
            ends = shift(sides[f], 127 - (8 * k + 2))
            e.append(jnp.where(lane == 127, ends, shift(x, -1)))
            w.append(jnp.where(lane == 0, ends, shift(x, 1)))
            n.append(jnp.where(last_row, rows_n[f][k : k + 1], shift(x, -1, 0)))
            s.append(jnp.where(first_row, rows_s[f][k : k + 1], shift(x, 1, 0)))
        flow_e = (now[2] + e[2]) * half_e
        flow_w = (now[2] + w[2]) * half_w
        flow_n = (now[3] + n[3]) * half_n
        flow_s = (now[3] + s[3]) * half_s
        out_e, in_e = jnp.maximum(flow_e, 0.0), jnp.minimum(flow_e, 0.0)
        in_w, out_w = jnp.maximum(flow_w, 0.0), jnp.minimum(flow_w, 0.0)
        out_n, in_n = jnp.maximum(flow_n, 0.0), jnp.minimum(flow_n, 0.0)
        in_s, out_s = jnp.maximum(flow_s, 0.0), jnp.minimum(flow_s, 0.0)
        kept = 1.0 - ((out_e - out_w) + (out_n - out_s))
        wet = k < depth
        new = []
        for f in range(2):
            x = now[f]
            total = (x * kept - (in_e * e[f] - in_w * w[f])) - (in_n * n[f] - in_s * s[f])
            if above is not None:
                flux = jnp.where(k + 1 < depth, MIXING * (above[f] - x), 0.0)
                total = total + flux
            if carried[f] is not None:
                total = total - carried[f]
            if above is not None:
                carried[f] = flux
            new.append(jnp.where(wet, total, 0.0))
        thick = 2.0 * VISCOSITY
        vis_e, vis_w, vis_n, vis_s = (thick * x for x in (half_e, half_w, half_n, half_s))
        kept = kept - ((vis_e + vis_w) + (vis_n + vis_s))
        in_e, in_w, in_n, in_s = vis_e - in_e, vis_w + in_w, vis_n - in_n, vis_s + in_s
        ua, va = (
            (now[f] * kept + (in_e * e[f] + in_w * w[f])) + (in_n * n[f] + in_s * s[f]) for f in (2, 3)
        )
        new.append(jnp.where(wet, cosine * ua + sine * va, 0.0))
        new.append(jnp.where(wet, cosine * va - sine * ua, 0.0))
        for f in range(4):
            write(f, k, new[f])
        now = above


def early_kernel(
    heat, salt, zonal, merid, depth_in, packed, angles, even_low, odd, even_up, near, mid_out
):
    lat, lon = position()
    lat_odd = lax.rem(lat, 2) == 1
    lon_odd = lax.rem(lon, 2) == 1
    fields = (heat, salt, zonal, merid)
    depth = depth_in[...]
    even_rows = jnp.where(is_late_even(lat, lon), even_up[...], even_low[...])
    odd_rows = odd[...]
    south_rows = jnp.where(lat_odd, even_rows, odd_rows)
    north_rows = jnp.where(lat_odd, odd_rows, even_rows)
    near_cols = near[...]
    west_cols = jnp.where(lon_odd, near_cols, 0.0)
    east_cols = jnp.where(lon_odd, 0.0, near_cols)
    cols, col_depth = column_groups(packed, depth, west_cols, east_cols)

    def write(f, k, value):
        mid_out[f, k] = value

    whole_step(
        lambda f, k: fields[f][k],
        cols,
        [south_rows[f * 16 : f * 16 + 16] for f in range(4)],
        [north_rows[f * 16 : f * 16 + 16] for f in range(4)],
        write,
        depth,
        depths_beside(depth, col_depth, south_rows[128:129], north_rows[128:129]),
        angles[0:32, :],
        angles[32:64, :],
    )


def step_kernel(
    mid, heat, salt, zonal, merid, depth_in, packed, angles, even_low, odd, even_up, near, near_up, far_edge, far,
    heat_out, salt_out, zonal_out, merid_out, turned, last, sems,
):
    lat, lon = position()
    lat_odd = lax.rem(lat, 2) == 1
    lon_odd = lax.rem(lon, 2) == 1
    at_top = lat == N_LAT - 1
    edge = is_edge_run(lat)
    late = is_upper(lon)
    fields = (heat, salt, zonal, merid)
    lane = lanes_of((ROWS, LANES))
    place = lane & 7
    level = (lane >> 3).astype(jnp.float32)
    lane1 = lanes_of((1, LANES))
    place1 = lane1 & 7
    depth = depth_in[...]
    cosine, sine = angles[0:32, :], angles[32:64, :]

    signs = jnp.where(jnp.logical_and(at_top, place1 >= 4), -1.0, 1.0)

    def swap_pair(x):
        return jnp.where(lane1 & 1 == 1, shift(x, 1), shift(x, -1)) * signs

    odd_rows = jnp.where(edge, far_edge[48:184, :], odd[...])
    beside = odd_rows[132:134]
    turned[...] = odd_rows

    @pl.when(at_top)
    def _():
        for at in range(0, 130, 16):
            part = reversed_lanes(odd_rows[at : min(at + 16, 130)])
            turned[at : min(at + 16, 130), :] = -part if at < 128 and at // 16 % 4 >= 2 else part

    even_rows = jnp.where(is_late_even(lat, lon), even_up[...], even_low[...])
    even_beside = jnp.where(late, near_up[40:42, :], even_rows[132:134])
    beside = jnp.where(late, near_up[42:44, :], beside)
    odd_info = odd_rows[130:132]
    odd_rows = turned[...]
    south_rows = jnp.where(lat_odd, even_rows, odd_rows)
    north_rows = jnp.where(lat_odd, odd_rows, even_rows)
    far_cols = jnp.where(edge, far_edge[0:48, :], far[...])
    near_cols = jnp.where(late, near_up[0:40, :], near[...])
    west_cols = jnp.where(lon_odd, near_cols, far_cols[0:40])
    east_cols = jnp.where(lon_odd, far_cols[0:40], near_cols)

    q = odd[128:136, :]
    q_west = jnp.where(at_top, swap_pair(q[3:4]), q[2:3])
    q_east = jnp.where(at_top, swap_pair(q[2:3]), q[3:4])
    q_depth = jnp.where(at_top, reversed_lanes(q[0:1]), q[0:1])
    far_even = far_cols[40:41]
    far_odd = jnp.where(edge, jnp.where(lon_odd, q_west, q_east), far_cols[41:42])
    far_odd_d = jnp.where(edge, q_depth, far_cols[43:44])
    near_even, near_even_d = even_beside[0:1], even_beside[1:2]
    near_odd = jnp.where(at_top, swap_pair(beside[0:1]), beside[0:1])
    near_odd_d = jnp.where(at_top, jnp.where(lane1 == 0, shift(beside[1:2], -1), shift(beside[1:2], 1)), beside[1:2])

    def near_depth(row):
        return jnp.where(lon_odd, row[:, 1:2], row[:, 0:1])

    def far_depth(row):
        return jnp.where(lon_odd, row[:, 0:1], row[:, 127:128])

    def by_side(even_part, odd_part):
        return jnp.where(lat_odd, even_part, odd_part), jnp.where(lat_odd, odd_part, even_part)

    def west_east(near_part, far_part):
        return jnp.where(lon_odd, near_part, far_part), jnp.where(lon_odd, far_part, near_part)

    near_s, near_n = by_side(near_even, near_odd)
    far_s, far_n = by_side(far_even, far_odd)
    (sw, se), (nw, ne) = west_east(near_s, far_s), west_east(near_n, far_n)
    near_sd, near_nd = by_side(near_depth(near_even_d), near_depth(near_odd_d))
    far_sd, far_nd = by_side(far_depth(far_cols[42:43]), far_depth(far_odd_d))
    corner_depth = [west_east(near_sd, far_sd), west_east(near_nd, far_nd)]
    odd_west = jnp.where(at_top, swap_pair(odd_info[1:2]), odd_info[0:1])
    odd_east = jnp.where(at_top, swap_pair(odd_info[0:1]), odd_info[1:2])
    own_sw, own_nw = by_side(even_rows[130:131], odd_west)
    own_se, own_ne = by_side(even_rows[131:132], odd_east)

    cols, col_depth = column_groups(packed, depth, west_cols, east_cols)
    cols_s, cols_n, corner_rows = [], [], []
    for out, w, e, own_w, own_e in ((cols_s, sw, se, own_sw, own_se), (cols_n, nw, ne, own_nw, own_ne)):
        for f in range(4):
            x = jnp.where(place1 == 5, shift(w, 4 - 2 * f), shift(e, 2 - 2 * f))
            x = jnp.where(place1 == 6, shift(own_w, 6 - 2 * f), x)
            out.append(jnp.where(place1 == 1, shift(own_e, -2 * f), x))
    for (w, e), own in zip(corner_depth, (south_rows[128:129], north_rows[128:129])):
        x = jnp.where(place1 == 5, w, e)
        x = jnp.where(place1 == 6, own[:, 0:1], x)
        corner_rows.append(jnp.where(place1 == 1, own[:, 127:128], x))

    wets = [
        as_wet(level < x)
        for x in (
            shift(col_depth, -1),
            shift(col_depth, 1),
            north_of(col_depth, corner_rows[1]),
            south_of(col_depth, corner_rows[0]),
        )
    ]
    cols_mid = five_point(
        cols,
        [shift(x, -1) for x in cols],
        [shift(x, 1) for x in cols],
        [north_of(x, y) for x, y in zip(cols, cols_n)],
        [south_of(x, y) for x, y in zip(cols, cols_s)],
        [shift(x, -8) for x in cols[:2]],
        [shift(x, 8) for x in cols[:2]],
        as_wet(level < col_depth),
        wets,
        as_wet(level + 1.0 < col_depth),
        as_wet(jnp.logical_and(lane >= 8, level - 1.0 < col_depth)),
        cosine,
        sine,
    )

    lane16 = lanes_of((LEVELS, LANES))
    sub16 = lax.broadcasted_iota(jnp.int32, (LEVELS, LANES), 0)
    lev16 = sub16.astype(jnp.float32)

    def one_row(c, n, s, ends, ends_d, d0, d_n, d_s, cos_row, sin_row):
        d_w = jnp.where(lane1 == 0, ends_d[0], shift(d0, 1))
        d_e = jnp.where(lane1 == 127, ends_d[1], shift(d0, -1))
        e, w = [], []
        for f in range(4):
            spread_out = jnp.broadcast_to(ends[f], (LEVELS, LANES))
            at_w = jnp.sum(jnp.where(lane16 == 8 * sub16 + 5, spread_out, 0.0), axis=1, keepdims=True)
            at_e = jnp.sum(jnp.where(lane16 == 8 * sub16 + 2, spread_out, 0.0), axis=1, keepdims=True)
            w.append(jnp.where(lane16 == 0, at_w, shift(c[f], 1)))
            e.append(jnp.where(lane16 == 127, at_e, shift(c[f], -1)))
        return five_point(
            c, e, w, n, s,
            [north_of(x, x[15:16]) for x in c[:2]],
            [south_of(x, x[0:1]) for x in c[:2]],
            as_wet(lev16 < d0),
            [as_wet(lev16 < x) for x in (d_e, d_w, d_n, d_s)],
            as_wet(lev16 + 1.0 < d0),
            as_wet(jnp.logical_and(sub16 >= 1, lev16 - 1.0 < d0)),
            cos_row,
            sin_row,
        )

    def of_rows(rows, d):
        at = 64 * d
        return [rows[at + f * 16 : at + f * 16 + 16] for f in range(4)]

    bottom = [x[:, 0, :] for x in fields]
    top = [x[:, ROWS - 1, :] for x in fields]
    south_mid = one_row(
        of_rows(south_rows, 0), bottom, of_rows(south_rows, 1), cols_s, corner_depth[0],
        south_rows[128:129], depth[0:1], south_rows[129:130], angles[64:65, :], angles[66:67, :],
    )
    north_mid = one_row(
        of_rows(north_rows, 0), of_rows(north_rows, 1), top, cols_n, corner_depth[1],
        north_rows[128:129], north_rows[129:130], depth[31:32], angles[65:66, :], angles[67:68, :],
    )

    def outer(top_part, bottom_part):
        return jnp.where(lat_odd, top_part, bottom_part)

    inner = [outer(x[:, ROWS - 2, :], x[:, 1, :]) for x in fields]
    beyond = of_rows(odd_rows, 0)
    inner_d, beyond_d = outer(depth[30:31], depth[1:2]), odd_rows[128:129]
    ends_d = outer(col_depth[31:32], col_depth[0:1])
    outer_mid = one_row(
        [outer(x, y) for x, y in zip(top, bottom)],
        [outer(x, y) for x, y in zip(beyond, inner)],
        [outer(x, y) for x, y in zip(inner, beyond)],
        [outer(x[31:32], x[0:1]) for x in cols],
        (ends_d[:, 5:6], ends_d[:, 2:3]),
        outer(depth[31:32], depth[0:1]),
        outer(beyond_d, inner_d),
        outer(inner_d, beyond_d),
        outer(cosine[31:32], cosine[0:1]),
        outer(sine[31:32], sine[0:1]),
    )

    row = lax.broadcasted_iota(jnp.int32, (ROWS, LANES), 0)
    redone_row = row == outer(ROWS - 1, 0)
    rim = jnp.logical_or(lane == 0, lane == 127)
    rims = [jnp.where(place == 1, x, shift(x, -4)) for x in cols_mid]

    def patched(f, k):
        x = jnp.where(rim, shift(rims[f], 127 - (8 * k + 1)), mid[f, k])
        return jnp.where(redone_row, outer_mid[f][k : k + 1], x)

    outs = (heat_out, salt_out, zonal_out, merid_out)
    copies = []

    def to_out(f, k, value):
        last[f, k] = value
        if k % CHUNK == CHUNK - 1:
            part = pl.ds(k + 1 - CHUNK, CHUNK)
            copy = pltpu.make_async_copy(last.at[f, part], outs[f].at[part], sems.at[f, k // CHUNK])
            copy.start()
            copies.append(copy)

    whole_step(
        patched,
        cols_mid,
        south_mid,
        north_mid,
        to_out,
        depth,
        depths_beside(depth, col_depth, south_rows[128:129], north_rows[128:129]),
        cosine,
        sine,
    )
    for copy in copies:
        copy.wait()


def shapes(*dims):
    return [jax.ShapeDtypeStruct(d, jnp.float32) for d in dims]


def call(kernel, outputs, *operands, scratch=(), held_in=True, held_out=True, grant=32, cost=False):
    vmem, hbm = pl.BlockSpec(memory_space=pltpu.VMEM), pl.BlockSpec(memory_space=pltpu.HBM)
    return pl.pallas_call(
        kernel,
        out_shape=shapes(*outputs),
        in_specs=[vmem if held_in else hbm] * len(operands),
        out_specs=[vmem if held_out else hbm] * len(outputs),
        scratch_shapes=list(scratch),
        cost_estimate=pl.CostEstimate(flops=30_000_000, bytes_accessed=2 << 20, transcendentals=0) if cost else None,
        compiler_params=pltpu.CompilerParams(vmem_limit_bytes=int(grant * 1024 * 1024)),
    )(*operands)


def angle_table():
    first = lax.axis_index("lat") * ROWS
    total = ROWS * N_LAT
    ids = jnp.concatenate([jnp.arange(ROWS), jnp.array([-1, ROWS])]) + first
    ids = jnp.where(ids >= total, 2 * total - 1 - ids, ids)
    angle = ROTATION * (2.0 * (ids.astype(jnp.float32) + 0.5) / total - 1.0)
    c, s = jnp.cos(angle), jnp.sin(angle)
    column = jnp.concatenate([c[:ROWS], s[:ROWS], c[ROWS:], s[ROWS:], jnp.zeros((4,), jnp.float32)])
    return jnp.broadcast_to(column[:, None], (72, LANES))


def on_device(heat, salt, zonal, merid, flag, tally):
    whole = (heat, salt, zonal, merid, flag, tally)
    size = (LEVELS, ROWS, LANES)
    pinned = [pltpu.with_memory_space_constraint(x, pltpu.HBM) for x in whole]
    *fields, depth, packed, info_top, info_bottom, col_near, col_far = call(
        pack_kernel,
        [size] * 4 + [(ROWS, LANES), (4, ROWS, LANES), (8, LANES), (8, LANES), (40, LANES), (40, LANES)],
        *pinned,
        scratch=[pltpu.VMEM((ROWS, LANES), jnp.int32)] * 2 + [pltpu.SemaphoreType.DMA((6,))],
        held_in=False,
    )
    near = send(col_near, near_lon, lambda lat, lon: not upper(lon) or lat == N_LAT - 1)
    rows = call(row_kernel, [(128, LANES)] * 3, *fields)
    row_low, row_odd, row_up = call(join_kernel, [(ROW_MSG, LANES)] * 3, *rows, info_top, info_bottom, near)
    even_low = send(row_low, even_lat, meets_even_early)
    odd = send(row_odd, odd_or_diagonal, lambda lat, lon: lat > 0)
    even_up = send(row_up, even_lat, lambda lat, lon: not meets_even_early(lat, lon))
    to_far, to_far_edge = call(
        relay_kernel, [(COL_MSG, LANES), (EDGE_MSG, LANES)], even_low, odd, even_up, col_far
    )
    far = send(to_far, far_lon, lambda lat, lon: not is_edge(lat))
    far_edge = send(to_far_edge, far_lon, lambda lat, lon: is_edge(lat))
    known = (*fields, depth, packed, angle_table(), even_low, odd, even_up, near)
    (mid,) = call(early_kernel, [(4,) + size], *known, cost=True)
    (to_near,) = call(near_kernel, [(COL_MSG, LANES)], even_low, odd, even_up, far_edge, col_near, mid)
    near_up = send(to_near, near_lon, lambda lat, lon: upper(lon))
    return tuple(
        call(
            step_kernel,
            [size] * 4,
            mid, *known, near_up, far_edge, far,
            scratch=[
                pltpu.VMEM((ROW_MSG, LANES), jnp.float32),
                pltpu.VMEM((4,) + size, jnp.float32),
                pltpu.SemaphoreType.DMA((4, LEVELS // CHUNK)),
            ],
            held_out=False,
        )
    )


def solution(mesh):
    field, column = P(None, "lat", "lon"), P("lat", "lon")
    return jax.shard_map(
        on_device,
        mesh=mesh,
        in_specs=(field,) * 4 + (column,) * 2,
        out_specs=(field,) * 4,
        check_vma=False,
    )
```
